256 devices in a mesh: grp: 8 (over x, z_lo), att: 32 (over y, z_hi, core).
Axes of the slice: x: 4, y: 4, z: 8 (z_hi: 4, z_lo: 2; z = z_hi * 2 + z_lo), core: 2. Of those that a mesh axis runs over, the one named last changes fastest.
Arguments:
- hidden_in: bfloat16 [1024, 8192], P(None, 'grp'), may hold values from -20 to 20
- queries: bfloat16 [1024, 8192], P(('grp', 'att')), may hold values from -100 to 100
- cache_key: bfloat16 [1024, 256, 1024], P(('grp', 'att')), may hold values from -5 to 5
- cache_value: bfloat16 [1024, 256, 1024], P(('grp', 'att')), may hold values from -6 to 6
- new_key: bfloat16 [1024, 1024], P(('grp', 'att')), may hold values from -6 to 6
- new_value: bfloat16 [1024, 1024], P(('grp', 'att')), may hold values from -6 to 6
- lengths: int32 [1024], P(('grp', 'att')), may hold values from 1 to 256, as said below
- out_weight: bfloat16 [8192, 8192], P('att', 'grp'), may hold values from -0.0625 to 0.0625
- norm_gain: float32 [8192], P('grp'), may hold values from 0.1 to 1.9
- w_gate: bfloat16 [8192, 28672], P('grp', 'att'), may hold values from -0.0625 to 0.0625
- w_up: bfloat16 [8192, 28672], P('grp', 'att'), may hold values from -0.0625 to 0.0625
- w_down: bfloat16 [28672, 8192], P('att', 'grp'), may hold values from -0.03125 to 0.03125
Outputs:
- layer_out: bfloat16 [1024, 8192], P('att', 'grp')
The draws below stay inside these ranges and needn't reach their ends.
Inputs may be any that keep to these rules, and one draw needn't show every extreme that they name: `lengths`: some row has 256 live slots and some row has one.
All inputs are finite; a program needn't handle non-finite values.
Results may differ from the reference program's by a relative error of at most 0.012.
Values may be sent and summed in bfloat16 or wider, within the bound.
No kernel may reach another device: no remote copies, remote signals or barrier semaphores. Data moves between devices by JAX's collectives and lax.ppermute only.
A program may use at most 128 MiB of HBM per device.

```python
import math
import jax
import jax.numpy as jnp
from jax import lax

D = 8192
FF = 28672
HQ = 64
KVH = 8
HD = 128
CTX = 256
ROWS = 1024


def first_keys(key):
    return jnp.clip(jax.random.normal(jax.random.fold_in(key, 11), (ROWS, KVH * HD), jnp.float32), -4.0, 4.0)


def draw_cache_key(key, part):
    first = first_keys(key)
    key = jax.random.fold_in(key, 1)
    others = jnp.clip(jax.random.normal(key, (ROWS, CTX, KVH * HD), jnp.float32), -4.0, 4.0)
    return others.at[:, 0].set(first).astype(jnp.bfloat16)


def draw_queries(key, part):
    key = jax.random.fold_in(key, 2)
    result = 2.5 * jnp.clip(jax.random.normal(key, (ROWS, HQ * HD), jnp.float32), -4.0, 4.0)
    return result.astype(jnp.bfloat16)


def draw_lengths(key, part):
    key = jax.random.fold_in(key, 3)
    live = jax.random.randint(key, (ROWS,), 1, CTX + 1, dtype=jnp.int32)
    return live.at[0].set(CTX).at[1].set(1)


def draw_hidden_in(key, part):
    key = jax.random.fold_in(key, 4)
    key_base, key_cols, key_rows = jax.random.split(key, 3)
    columns = jnp.arange(D, dtype=jnp.float32) / D
    col_scale = jnp.exp(math.log(3.0) * columns + jax.random.uniform(key_cols, (D,), jnp.float32, 0.0, math.log(1.5)))
    base = jnp.clip(jax.random.normal(key_base, (ROWS, D), jnp.float32), -4.0, 4.0)
    row_scale = jnp.exp(jax.random.uniform(key_rows, (ROWS, 1), jnp.float32, math.log(0.1), 0.0))
    return (base * row_scale * col_scale).astype(jnp.bfloat16)


def steps_of(own_key, shape, cuts, smallest, top_value):
    gain = 1.0
    for dim, blocks in cuts:
        heights = jax.random.uniform(jax.random.fold_in(jax.random.fold_in(own_key, 6), dim), (blocks,), jnp.float32, smallest / len(cuts), top_value / len(cuts))
        gain = gain * jnp.repeat(jnp.exp(heights), shape[dim] // blocks).reshape((-1,) + (1,) * (len(shape) - 1 - dim))
    return gain


def bell_draw(stream_key, extent, scale, most, shards=(), held_as=jnp.bfloat16):
    array = scale * jax.random.normal(stream_key, extent, jnp.float32)
    if shards:
        array = array * steps_of(stream_key, extent, shards, -0.22, 0.18)
    return jnp.clip(array, -most, most).astype(held_as)


def setup_inputs(seed: int = 0) -> dict:
    key_of = jax.random.split(jax.random.key(seed), 13)
    return {
        "hidden_in": draw_hidden_in(jax.random.fold_in(key_of[12], 71), 0),
        "queries": draw_queries(jax.random.fold_in(key_of[12], 71), 0),
        "cache_key": draw_cache_key(jax.random.fold_in(key_of[12], 71), 0),
        "cache_value": bell_draw(key_of[3], (ROWS, CTX, KVH * HD), 1.0, 6.0, ((0, 256),)),
        "new_key": bell_draw(key_of[4], (ROWS, KVH * HD), 1.0, 6.0, ((0, 256),)),
        "new_value": bell_draw(key_of[5], (ROWS, KVH * HD), 1.0, 6.0, ((0, 256),)),
        "lengths": draw_lengths(jax.random.fold_in(key_of[12], 71), 0),
        "out_weight": bell_draw(key_of[7], (HQ * HD, D), (HQ * HD) ** -0.5, 0.0625, ((0, 32), (1, 8))),
        "norm_gain": jnp.clip(1.0 + 0.18 * jax.random.normal(key_of[8], (D,), jnp.float32), 0.1, 1.9),
        "w_gate": bell_draw(key_of[9], (D, FF), D ** -0.5, 0.0625, ((0, 8), (1, 32))),
        "w_up": bell_draw(key_of[10], (D, FF), D ** -0.5, 0.0625, ((0, 8), (1, 32))),
        "w_down": bell_draw(key_of[11], (FF, D), FF ** -0.5, 0.03125, ((0, 32), (1, 8))),
    }


def attend_row(packed):
    query_row, key_rows, value_rows, key_new, value_new, live = packed
    scale_factor = 1.0 / jnp.sqrt(jnp.float32(HD))
    query_heads = query_row.astype(jnp.float32).reshape(KVH, HQ // KVH, HD)
    key_heads = key_rows.astype(jnp.float32).reshape(CTX, KVH, HD)
    value_heads = value_rows.astype(jnp.float32).reshape(CTX, KVH, HD)
    scores = jnp.einsum('kgd,pkd->kgp', query_heads, key_heads) * scale_factor
    score_new = jnp.einsum('kgd,kd->kg', query_heads, key_new.astype(jnp.float32).reshape(KVH, HD)) * scale_factor
    valid = jnp.arange(CTX, dtype=jnp.int32) < live
    scores = jnp.where(valid[None, None, :], scores, -jnp.inf)
    top_score = jnp.maximum(lax.optimization_barrier(jnp.max(scores, axis=-1)), score_new)
    weights = jnp.exp(scores - top_score[..., None])
    weight_new = jnp.exp(score_new - top_score)
    total = lax.optimization_barrier(jnp.sum(weights, axis=-1)) + weight_new
    weights_low = lax.optimization_barrier(weights.astype(jnp.bfloat16)).astype(jnp.float32)
    new_low = lax.optimization_barrier(weight_new.astype(jnp.bfloat16)).astype(jnp.float32)
    summed = jnp.einsum('kgp,pkd->kgd', weights_low, value_heads)
    summed = summed + new_low[..., None] * value_new.astype(jnp.float32).reshape(KVH, 1, HD)
    return (summed / total[..., None]).astype(jnp.bfloat16).reshape(HQ * HD)

def reference(hidden_in, queries, cache_key, cache_value, new_key, new_value, lengths, out_weight, norm_gain, w_gate, w_up, w_down):
    attended = lax.map(attend_row, (queries, cache_key, cache_value, new_key, new_value, lengths))
    mixed = hidden_in.astype(jnp.float32) + jnp.dot(attended, out_weight, preferred_element_type=jnp.float32)
    inv_rms = lax.rsqrt(lax.optimization_barrier(jnp.mean(mixed * mixed, axis=1)) + 1e-05)
    normed = (mixed * norm_gain).astype(jnp.bfloat16)
    gate = jnp.dot(normed, w_gate, preferred_element_type=jnp.float32) * inv_rms[:, None]
    up_proj = jnp.dot(normed, w_up, preferred_element_type=jnp.float32) * inv_rms[:, None]
    hidden = (jax.nn.silu(gate) * up_proj).astype(jnp.bfloat16)
    return (mixed + jnp.dot(hidden, w_down, preferred_element_type=jnp.float32)).astype(jnp.bfloat16)
```

```python
import jax
import jax.numpy as jnp
import numpy as np
from jax import lax
from jax.experimental import pallas as pl
from jax.experimental.pallas import tpu as pltpu
from jax.sharding import Mesh
from jax.sharding import PartitionSpec as P

NAMES = ("x", "l", "y", "z", "core")
SIZES = (4, 2, 4, 4, 2)
GRP, ATT = ("x", "l"), ("y", "z", "core")
VMEM = pl.BlockSpec(memory_space=pltpu.VMEM)
SMEM = pl.BlockSpec(memory_space=pltpu.SMEM)
ANY = pl.BlockSpec(memory_space=pl.ANY)
STEP = 256

D = 8192
HQ = 64
KVH = 8
HD = 128


def attend(queries, cache_key, cache_value, new_key, new_value, lengths):
    row_count = queries.shape[0]
    slot_count = cache_key.shape[1]
    scale_factor = 1.0 / jnp.sqrt(jnp.float32(HD))
    query_heads = queries.reshape(row_count, KVH, HQ // KVH, HD)
    key_heads = cache_key.reshape(row_count, slot_count, KVH, HD)
    value_heads = cache_value.reshape(row_count, slot_count, KVH, HD)
    scores = (
        jnp.einsum("rkgd,rpkd->rkgp", query_heads, key_heads, preferred_element_type=jnp.float32)
        * scale_factor
    )
    score_new = (
        jnp.einsum(
            "rkgd,rkd->rkg",
            query_heads,
            new_key.reshape(row_count, KVH, HD),
            preferred_element_type=jnp.float32,
        )
        * scale_factor
    )
    valid = jnp.arange(slot_count, dtype=jnp.int32)[None, :] < lengths[:, None]
    scores = jnp.where(valid[:, None, None, :], scores, -jnp.inf)
    top_score = jnp.maximum(jnp.max(scores, axis=-1), score_new)
    weights = jnp.exp(scores - top_score[..., None])
    weight_new = jnp.exp(score_new - top_score)
    total = jnp.sum(weights, axis=-1) + weight_new
    summed = jnp.einsum(
        "rkgp,rpkd->rkgd",
        weights.astype(jnp.bfloat16),
        value_heads,
        preferred_element_type=jnp.float32,
    )
    new_low = weight_new.astype(jnp.bfloat16).astype(jnp.float32)
    summed = summed + new_low[..., None] * new_value.astype(jnp.float32).reshape(
        row_count, KVH, 1, HD
    )
    return (summed / total[..., None]).astype(jnp.bfloat16).reshape(row_count, HQ * HD)


def activate(gate_sum, up_sum, square_sum):
    inv_rms = lax.rsqrt(square_sum / D + 1e-05)
    gate = gate_sum * inv_rms[:, None]
    up_proj = up_sum * inv_rms[:, None]
    return (jax.nn.silu(gate) * up_proj).astype(jnp.bfloat16)


def places():
    table = np.zeros((256, 13), np.int32)
    for device in range(256):
        x, l, y, core = device >> 6, (device >> 5) & 1, (device >> 3) & 3, device & 1
        table[device, :8] = [(l ^ b) * 4 + (x ^ j) for j in range(4) for b in range(2)]
        table[device, 8:12] = [(y + t) % 4 for t in range(4)]
        table[device, 12] = core
    return table


def swap(block, axis):
    return lax.ppermute(block, axis, [(0, 1), (1, 0)])


def ring_from(block, axis, shift):
    return lax.ppermute(block, axis, [((i + shift) % 4, i) for i in range(4)])


def ring_to(block, axis, shift):
    return lax.ppermute(block, axis, [(i, (i + shift) % 4) for i in range(4)])


def spread(block, step):
    perm = []
    for x in range(4):
        for y in range(4):
            for core in range(2):
                target = (((y // 2) * 2 + core) ^ step, x, y % 2)
                perm.append(((x * 4 + y) * 2 + core, (target[0] * 4 + target[1]) * 2 + target[2]))
    return lax.ppermute(block, ("x", "y", "core"), perm)


def params(mebibytes, flops, nbytes):
    return dict(
        compiler_params=pltpu.CompilerParams(vmem_limit_bytes=mebibytes << 20),
        cost_estimate=pl.CostEstimate(flops=flops, bytes_accessed=nbytes, transcendentals=0),
    )


def steps(width):
    return [(n, min(STEP, width - n)) for n in range(0, width, STEP)]


def start_all(copies):
    for copy in copies:
        copy.start()
    return copies


def wait_all(copies):
    for copy in copies:
        copy.wait()


def project_kernel(place_ref, *refs):
    pieces, own, other, others = refs[:4], refs[4:8], refs[8], refs[9]
    out_ref, rows_ref, held_ref, row_sems, held_sems = refs[10:]
    step = pieces[0].shape[0] // 2
    row_copies = start_all(
        [
            pltpu.make_async_copy(
                pieces[j].at[pl.ds(b * step, step), :],
                rows_ref.at[pl.ds(pl.multiple_of(place_ref[2 * j + b] * step, step), step), :],
                row_sems.at[2 * j + b],
            )
            for j in range(4)
            for b in range(2)
        ]
    )
    depth, width = own[0].shape
    held_copies = []
    for t in range(4):
        for b in range(2):
            source = own[t] if b == 0 else (other if t == 0 else others.at[pl.ds((t - 1) * depth, depth), :])
            start = (2 * place_ref[8 + t] + (place_ref[12] if b == 0 else 1 - place_ref[12])) * depth
            held = held_ref.at[pl.ds(pl.multiple_of(start, depth), depth), :]
            held_copies.append(pltpu.make_async_copy(source, held, held_sems.at[2 * t + b]))
    start_all(held_copies)
    wait_all(row_copies)
    wait_all(held_copies)
    for n, size in steps(width):
        out_ref[:, n : n + size] = jnp.dot(
            rows_ref[...], held_ref[:, n : n + size], preferred_element_type=jnp.float32
        ).astype(out_ref.dtype)


def project(place, pieces, own, other, others):
    count, depth = 4 * pieces[0].shape[0], pieces[0].shape[1]
    width = other.shape[1]
    return pl.pallas_call(
        project_kernel,
        in_specs=[SMEM] + [ANY] * 10,
        out_specs=VMEM,
        out_shape=jax.ShapeDtypeStruct((count, width), jnp.bfloat16),
        scratch_shapes=[
            pltpu.VMEM((count, depth), jnp.bfloat16),
            pltpu.VMEM((depth, width), jnp.bfloat16),
            pltpu.SemaphoreType.DMA((8,)),
            pltpu.SemaphoreType.DMA((8,)),
        ],
        name="project",
        **params(12, 2 * count * depth * width, 2 * (depth * width + count * (depth + width))),
    )(place, *pieces, *own, other, others)


def gate_up_kernel(gain_ref, *refs):
    pieces, weights = refs[:-9], refs[-9:-5]
    out_ref, rows_ref, held_ref, row_sems, held_sems = refs[-5:]
    step = pieces[0].shape[0]
    width = weights[0].shape[1]
    row_copies = start_all(
        [
            pltpu.make_async_copy(piece, rows_ref.at[pl.ds(t * step, step), :], row_sems.at[t])
            for t, piece in enumerate(pieces)
        ]
    )
    held_copies = start_all(
        [pltpu.make_async_copy(weights[j], held_ref.at[j], held_sems.at[j]) for j in range(4)]
    )
    inverse = 1.0 / gain_ref[...]
    part = 64
    lane = lax.broadcasted_iota(jnp.int32, (part, 128), 1)
    wait_all(row_copies)
    for t in range(0, rows_ref.shape[0], part):
        mixed = rows_ref[t : t + part, :].astype(jnp.float32) * inverse
        squares = jnp.sum(mixed * mixed, axis=1, keepdims=True)
        high = squares.astype(jnp.bfloat16).astype(jnp.float32)
        columns = jnp.where(lane == 0, high, jnp.where(lane == 1, squares - high, 0.0))
        out_ref[t : t + part, 4 * width :] = columns.astype(out_ref.dtype)
    for j in range(4):
        held_copies[j].wait()
        for n, size in steps(width):
            product = jnp.dot(rows_ref[...], held_ref[j, :, n : n + size], preferred_element_type=jnp.float32)
            out_ref[:, j * width + n : j * width + n + size] = product.astype(out_ref.dtype)


def gate_up(gain, pieces, weights):
    count, depth = len(pieces) * pieces[0].shape[0], pieces[0].shape[1]
    width = weights[0].shape[1]
    return pl.pallas_call(
        gate_up_kernel,
        in_specs=[VMEM] + [ANY] * (len(pieces) + 4),
        out_specs=VMEM,
        out_shape=jax.ShapeDtypeStruct((count, 4 * width + 128), jnp.bfloat16),
        scratch_shapes=[
            pltpu.VMEM((count, depth), jnp.bfloat16),
            pltpu.VMEM((4, depth, width), jnp.bfloat16),
            pltpu.SemaphoreType.DMA((len(pieces),)),
            pltpu.SemaphoreType.DMA((4,)),
        ],
        name="gate_up",
        **params(20, 8 * count * depth * width, 2 * (count * depth + 4 * depth * width + 4 * count * width)),
    )(gain, *pieces, *weights)


def down_kernel(hidden_ref, own, other, *refs):
    outs, rows_ref, held_ref, row_sem, held_sems = refs[:4], refs[4], refs[5], refs[6], refs[7]
    depth, width = own.shape
    row_copy = pltpu.make_async_copy(hidden_ref, rows_ref, row_sem.at[0])
    row_copy.start()
    held_copies = start_all(
        [
            pltpu.make_async_copy(weight, held_ref.at[pl.ds(i * depth, depth), :], held_sems.at[i])
            for i, weight in enumerate((own, other))
        ]
    )
    row_copy.wait()
    share = outs[0].shape[0]
    first = share // 8
    near = rows_ref[:, :first].reshape(share, 2 * depth)
    far = rows_ref[:, first:].reshape(3 * share, 2 * depth)
    wait_all(held_copies)
    for n, size in steps(width):
        columns = held_ref[:, n : n + size]
        product = jnp.dot(far, columns, preferred_element_type=jnp.float32)
        for t in range(3):
            outs[t + 1][:, n : n + size] = product[t * share : (t + 1) * share].astype(outs[t + 1].dtype)
        product = jnp.dot(near, columns, preferred_element_type=jnp.float32)
        outs[0][:, n : n + size] = product.astype(outs[0].dtype)


def down(hidden, weights):
    count = hidden.shape[0] * hidden.shape[1]
    depth, width = weights[0].shape
    return pl.pallas_call(
        down_kernel,
        in_specs=[ANY] * 3,
        out_specs=[VMEM] * 4,
        out_shape=[jax.ShapeDtypeStruct((count // 4, width), jnp.bfloat16)] * 4,
        scratch_shapes=[
            pltpu.VMEM(hidden.shape, jnp.bfloat16),
            pltpu.VMEM((2 * depth, width), jnp.bfloat16),
            pltpu.SemaphoreType.DMA((1,)),
            pltpu.SemaphoreType.DMA((2,)),
        ],
        name="down",
        **params(16, 4 * count * depth * width, 2 * (2 * count * depth + 2 * depth * width + count * width)),
    )(hidden, *weights)


def add_up(pieces):
    total = pieces[0].astype(jnp.float32)
    for piece in pieces[1:]:
        total = total + piece.astype(jnp.float32)
    return total


def exchange(pieces, axis):
    return lax.all_to_all(pieces, axis, split_axis=0, concat_axis=0, tiled=True)


def scatter_sum(partial, axis):
    parts = lax.axis_size(axis)
    pieces = partial.reshape(parts, partial.shape[0] // parts, partial.shape[1])
    return jnp.sum(exchange(pieces, axis).astype(jnp.float32), axis=0)


def gather(rows, axis):
    return exchange(jnp.broadcast_to(rows[None], (lax.axis_size(axis),) + rows.shape), axis)


def body(
    hidden_in,
    queries,
    cache_key,
    cache_value,
    new_key,
    new_value,
    lengths,
    out_weight,
    norm_gain,
    w_gate,
    w_up,
    w_down,
):
    device = lax.axis_index(GRP + ATT)
    place = lax.dynamic_slice_in_dim(jnp.asarray(places()), device, 1, 0)[0]
    out_own = [out_weight] + [ring_from(out_weight, "y", t) for t in (1, 2, 3)]
    out_other = swap(out_weight, "core")

    attended = attend(queries, cache_key, cache_value, new_key, new_value, lengths)
    count = attended.shape[0]
    slots = attended.reshape(count, 4, 4, -1).transpose(2, 0, 1, 3).reshape(4, count, -1)
    block = exchange(slots, "z").reshape(4 * count, -1)
    block = jnp.concatenate([block, swap(block, "l")], axis=0)
    block, *out_own[1:] = lax.optimization_barrier((block, *out_own[1:]))
    out_others = swap(jnp.concatenate(out_own[1:], axis=0), "core")
    pieces = [spread(block, step) for step in range(4)]
    partial = project(place, pieces, out_own, out_other, out_others)
    partial, *late = lax.optimization_barrier((partial, w_gate, w_up))
    gate_other, up_other = [swap(w, "core") for w in late]

    share = hidden_in.shape[0] // 32
    own_in = lax.dynamic_slice_in_dim(hidden_in, (device & 31) * share, share, 0)
    own_in = own_in.reshape(4, 2, count, -1).transpose(1, 0, 2, 3).reshape(share, -1)
    mixed = own_in.astype(jnp.float32) + scatter_sum(partial, "z")
    normed = (mixed * norm_gain).astype(jnp.bfloat16)
    normed, gate_other, up_other = lax.optimization_barrier((normed, gate_other, up_other))

    block = jnp.concatenate([normed] + [ring_from(normed, "z", t) for t in (1, 2, 3)], axis=0)
    block, late = lax.optimization_barrier((block, w_down))
    down_other = swap(late, "core")
    pieces = [ring_from(block, "y", t) for t in (1, 2, 3)]
    weights = [w_gate, w_up, gate_other, up_other]
    summed = [scatter_sum(gate_up(norm_gain[None, :], part, weights), GRP) for part in ([block], pieces)]
    summed = jnp.concatenate(summed, axis=0)
    width = w_gate.shape[1]
    square_sum = summed[:, 4 * width] + summed[:, 4 * width + 1]
    hidden = jnp.concatenate(
        [
            activate(summed[:, i * width : (i + 1) * width], summed[:, (i + 1) * width : (i + 2) * width], square_sum)
            for i in (0, 2)
        ],
        axis=1,
    )
    parts = down(gather(hidden, GRP), [w_down, down_other])
    total = add_up([parts[0]] + [ring_to(parts[t], "y", t) for t in (1, 2, 3)])
    parts = [total[t * share : (t + 1) * share] for t in range(4)]
    total = add_up([parts[0]] + [ring_to(parts[t].astype(jnp.bfloat16), "z", t) for t in (1, 2, 3)])
    layer_out = (mixed + total).astype(jnp.bfloat16)
    return layer_out.reshape(2, 4, count, -1).transpose(1, 0, 2, 3).reshape(share, -1)


def solution(mesh):
    fine = Mesh(mesh.devices.reshape(SIZES), NAMES)
    rows = P(GRP + ATT)
    in_specs = (
        P(None, GRP),
        rows,
        rows,
        rows,
        rows,
        rows,
        rows,
        P(ATT, GRP),
        P(GRP),
        P(GRP, ATT),
        P(GRP, ATT),
        P(ATT, GRP),
    )
    out_specs = P(ATT, GRP)
    return jax.shard_map(body, mesh=fine, in_specs=in_specs, out_specs=out_specs, check_vma=False)
```

```python
import jax
import jax.numpy as jnp
import numpy as np
from jax import lax
from jax.experimental import pallas as pl
from jax.experimental.pallas import tpu as pltpu
from jax.sharding import Mesh
from jax.sharding import PartitionSpec as P

NAMES = ("x", "l", "y", "z", "core")
SIZES = (4, 2, 4, 4, 2)
GRP, ATT = ("x", "l"), ("y", "z", "core")
VMEM = pl.BlockSpec(memory_space=pltpu.VMEM)
SMEM = pl.BlockSpec(memory_space=pltpu.SMEM)
ANY = pl.BlockSpec(memory_space=pl.ANY)
HBM = pl.BlockSpec(memory_space=pltpu.HBM)
STEP = 256

D = 8192
HQ = 64
KVH = 8
HD = 128


def attend(queries, cache_key, cache_value, new_key, new_value, lengths):
    row_count = queries.shape[0]
    slot_count = cache_key.shape[1]
    scale_factor = 1.0 / jnp.sqrt(jnp.float32(HD))
    query_heads = queries.reshape(row_count, KVH, HQ // KVH, HD)
    key_heads = cache_key.reshape(row_count, slot_count, KVH, HD)
    value_heads = cache_value.reshape(row_count, slot_count, KVH, HD)
    scores = (
        jnp.einsum("rkgd,rpkd->rkgp", query_heads, key_heads, preferred_element_type=jnp.float32)
        * scale_factor
    )
    score_new = (
        jnp.einsum(
            "rkgd,rkd->rkg",
            query_heads,
            new_key.reshape(row_count, KVH, HD),
            preferred_element_type=jnp.float32,
        )
        * scale_factor
    )
    valid = jnp.arange(slot_count, dtype=jnp.int32)[None, :] < lengths[:, None]
    scores = jnp.where(valid[:, None, None, :], scores, -jnp.inf)
    top_score = jnp.maximum(jnp.max(scores, axis=-1), score_new)
    weights = jnp.exp(scores - top_score[..., None])
    weight_new = jnp.exp(score_new - top_score)
    total = jnp.sum(weights, axis=-1) + weight_new
    summed = jnp.einsum(
        "rkgp,rpkd->rkgd",
        weights.astype(jnp.bfloat16),
        value_heads,
        preferred_element_type=jnp.float32,
    )
    new_low = weight_new.astype(jnp.bfloat16).astype(jnp.float32)
    summed = summed + new_low[..., None] * new_value.astype(jnp.float32).reshape(
        row_count, KVH, 1, HD
    )
    return (summed / total[..., None]).astype(jnp.bfloat16).reshape(row_count, HQ * HD)


def activate(gate_sum, up_sum, square_sum):
    inv_rms = lax.rsqrt(square_sum / D + 1e-05)
    gate = gate_sum * inv_rms[:, None]
    up_proj = up_sum * inv_rms[:, None]
    return (jax.nn.silu(gate) * up_proj).astype(jnp.bfloat16)


def places():
    table = np.zeros((256, 17), np.int32)
    for device in range(256):
        x, l, y, core = device >> 6, (device >> 5) & 1, (device >> 3) & 3, device & 1
        table[device, :8] = [(l ^ b) * 4 + (x ^ j) for j in range(4) for b in range(2)]
        table[device, 8:12] = [(y + t) % 4 for t in range(4)]
        table[device, 12] = core
        table[device, 13:] = [((device >> 1) + t) % 4 for t in range(4)]
    return table


def swap(block, axis):
    return lax.ppermute(block, axis, [(0, 1), (1, 0)])


def ring_from(block, axis, shift):
    return lax.ppermute(block, axis, [((i + shift) % 4, i) for i in range(4)])


def ring_to(block, axis, shift):
    return lax.ppermute(block, axis, [(i, (i + shift) % 4) for i in range(4)])


def spread(block, step):
    perm = []
    for x in range(4):
        for y in range(4):
            for core in range(2):
                target = (((y // 2) * 2 + core) ^ step, x, y % 2)
                perm.append(((x * 4 + y) * 2 + core, (target[0] * 4 + target[1]) * 2 + target[2]))
    return lax.ppermute(block, ("x", "y", "core"), perm)


def params(mebibytes, flops, nbytes):
    return dict(
        compiler_params=pltpu.CompilerParams(vmem_limit_bytes=mebibytes << 20),
        cost_estimate=pl.CostEstimate(flops=flops, bytes_accessed=nbytes, transcendentals=0),
    )


def steps(width):
    return [(n, min(STEP, width - n)) for n in range(0, width, STEP)]


def start_all(copies):
    for copy in copies:
        copy.start()
    return copies


def wait_all(copies):
    for copy in copies:
        copy.wait()


def project_kernel(place_ref, *refs):
    pieces, own, other, others = refs[:4], refs[4:8], refs[8], refs[9]
    outs, rows_ref, held_ref, total_ref, row_sems, held_sems = refs[10:14], *refs[14:]
    step = pieces[0].shape[0] // 2
    row_copies = start_all(
        [
            pltpu.make_async_copy(
                pieces[j].at[pl.ds(b * step, step), :],
                rows_ref.at[pl.ds(pl.multiple_of(place_ref[2 * j + b] * step, step), step), :],
                row_sems.at[2 * j + b],
            )
            for j in range(4)
            for b in range(2)
        ]
    )
    depth, width = own[0].shape
    held_copies = []
    for t in range(4):
        for b in range(2):
            source = own[t] if b == 0 else (other if t == 0 else others.at[pl.ds((t - 1) * depth, depth), :])
            start = (2 * place_ref[8 + t] + (place_ref[12] if b == 0 else 1 - place_ref[12])) * depth
            held = held_ref.at[pl.ds(pl.multiple_of(start, depth), depth), :]
            held_copies.append(pltpu.make_async_copy(source, held, held_sems.at[2 * t + b]))
    start_all(held_copies)
    wait_all(row_copies)
    wait_all(held_copies)
    for n, size in steps(width):
        total_ref[:, n : n + size] = jnp.dot(
            rows_ref[...], held_ref[:, n : n + size], preferred_element_type=jnp.float32
        )
    share = outs[0].shape[0]
    for t in range(4):
        start = pl.multiple_of(place_ref[13 + t] * share, share)
        outs[t][...] = total_ref[pl.ds(start, share), :].astype(outs[t].dtype)


def project(place, pieces, own, other, others):
    count, depth = 4 * pieces[0].shape[0], pieces[0].shape[1]
    width = other.shape[1]
    return pl.pallas_call(
        project_kernel,
        in_specs=[SMEM] + [ANY] * 4 + [HBM] * 6,
        out_specs=[VMEM] * 4,
        out_shape=[
            jax.ShapeDtypeStruct((count // 4, width), jnp.float32 if t == 0 else jnp.bfloat16) for t in range(4)
        ],
        scratch_shapes=[
            pltpu.VMEM((count, depth), jnp.bfloat16),
            pltpu.VMEM((depth, width), jnp.bfloat16),
            pltpu.VMEM((count, width), jnp.float32),
            pltpu.SemaphoreType.DMA((8,)),
            pltpu.SemaphoreType.DMA((8,)),
        ],
        name="project",
        **params(12, 2 * count * depth * width, 2 * (depth * width + count * (depth + width))),
    )(place, *pieces, *own, other, others)


def gate_up_kernel(gain_ref, *refs):
    pieces, weights = refs[:-11], refs[-11:-7]
    sent_ref, rows_ref, held_ref, out_ref, row_sems, held_sems, out_sems = refs[-7:]
    step = pieces[0].shape[0]
    width = weights[0].shape[1]
    row_copies = start_all(
        [
            pltpu.make_async_copy(piece, rows_ref.at[pl.ds(t * step, step), :], row_sems.at[t])
            for t, piece in enumerate(pieces)
        ]
    )
    held_copies = start_all(
        [pltpu.make_async_copy(weights[j], held_ref.at[j], held_sems.at[j]) for j in range(4)]
    )
    inverse = 1.0 / gain_ref[...]
    part = 64
    lane = lax.broadcasted_iota(jnp.int32, (part, 128), 1)
    wait_all(row_copies)
    for t in range(0, rows_ref.shape[0], part):
        mixed = rows_ref[t : t + part, :].astype(jnp.float32) * inverse
        squares = jnp.sum(mixed * mixed, axis=1, keepdims=True)
        high = squares.astype(jnp.bfloat16).astype(jnp.float32)
        columns = jnp.where(lane == 0, high, jnp.where(lane == 1, squares - high, 0.0))
        out_ref[t : t + part, 4 * width :] = columns.astype(out_ref.dtype)
    out_copies = []
    for j in range(4):
        held_copies[j].wait()
        for n, size in steps(width):
            product = jnp.dot(rows_ref[...], held_ref[j, :, n : n + size], preferred_element_type=jnp.float32)
            out_ref[:, j * width + n : j * width + n + size] = product.astype(out_ref.dtype)
        done = pl.ds(j * width, width if j < 3 else width + 128)
        out_copies += start_all([pltpu.make_async_copy(out_ref.at[:, done], sent_ref.at[:, done], out_sems.at[j])])
    wait_all(out_copies)


def gate_up(gain, pieces, weights):
    count, depth = len(pieces) * pieces[0].shape[0], pieces[0].shape[1]
    width = weights[0].shape[1]
    return pl.pallas_call(
        gate_up_kernel,
        in_specs=[VMEM] + [ANY] * len(pieces) + [HBM] * 4,
        out_specs=HBM,
        out_shape=jax.ShapeDtypeStruct((count, 4 * width + 128), jnp.bfloat16),
        scratch_shapes=[
            pltpu.VMEM((count, depth), jnp.bfloat16),
            pltpu.VMEM((4, depth, width), jnp.bfloat16),
            pltpu.VMEM((count, 4 * width + 128), jnp.bfloat16),
            pltpu.SemaphoreType.DMA((len(pieces),)),
            pltpu.SemaphoreType.DMA((4,)),
            pltpu.SemaphoreType.DMA((4,)),
        ],
        name="gate_up",
        **params(20, 8 * count * depth * width, 2 * (count * depth + 4 * depth * width + 4 * count * width)),
    )(gain, *pieces, *weights)


def down_kernel(hidden_ref, own, other, *refs):
    outs, rows_ref, held_ref, row_sem, held_sems = refs[:4], refs[4], refs[5], refs[6], refs[7]
    depth, width = own.shape
    row_copy = pltpu.make_async_copy(hidden_ref, rows_ref, row_sem.at[0])
    row_copy.start()
    held_copies = start_all(
        [
            pltpu.make_async_copy(weight, held_ref.at[pl.ds(i * depth, depth), :], held_sems.at[i])
            for i, weight in enumerate((own, other))
        ]
    )
    row_copy.wait()
    share = outs[0].shape[0]
    first = hidden_ref.shape[1] // 2
    near = rows_ref[:, :first].reshape(2 * share, 2 * depth)
    far = rows_ref[:, first:].reshape(2 * share, 2 * depth)
    wait_all(held_copies)
    for n, size in steps(width):
        columns = held_ref[:, n : n + size]
        for i, rows in enumerate((near, far)):
            product = jnp.dot(rows, columns, preferred_element_type=jnp.float32)
            for t in range(2):
                out_ref = outs[2 * i + t]
                out_ref[:, n : n + size] = product[t * share : (t + 1) * share].astype(out_ref.dtype)


def down(hidden, weights):
    count = hidden.shape[0] * hidden.shape[1]
    depth, width = weights[0].shape
    return pl.pallas_call(
        down_kernel,
        in_specs=[ANY] + [HBM] * 2,
        out_specs=[VMEM] * 4,
        out_shape=[jax.ShapeDtypeStruct((count // 4, width), jnp.bfloat16)] * 4,
        scratch_shapes=[
            pltpu.VMEM(hidden.shape, jnp.bfloat16),
            pltpu.VMEM((2 * depth, width), jnp.bfloat16),
            pltpu.SemaphoreType.DMA((1,)),
            pltpu.SemaphoreType.DMA((2,)),
        ],
        name="down",
        **params(16, 4 * count * depth * width, 2 * (2 * count * depth + 2 * depth * width + count * width)),
    )(hidden, *weights)


def add_up(pieces):
    total = pieces[0].astype(jnp.float32)
    for piece in pieces[1:]:
        total = total + piece.astype(jnp.float32)
    return total


def exchange(pieces, axis):
    return lax.all_to_all(pieces, axis, split_axis=0, concat_axis=0, tiled=True)


def scatter_sum(partial, axis):
    parts = lax.axis_size(axis)
    pieces = partial.reshape(parts, partial.shape[0] // parts, partial.shape[1])
    return jnp.sum(exchange(pieces, axis).astype(jnp.float32), axis=0)


def gather(rows, axis):
    return exchange(jnp.broadcast_to(rows[None], (lax.axis_size(axis),) + rows.shape), axis)


def body(
    hidden_in,
    queries,
    cache_key,
    cache_value,
    new_key,
    new_value,
    lengths,
    out_weight,
    norm_gain,
    w_gate,
    w_up,
    w_down,
):
    device = lax.axis_index(GRP + ATT)
    place = lax.dynamic_slice_in_dim(jnp.asarray(places()), device, 1, 0)[0]
    out_own = [out_weight] + [ring_from(out_weight, "y", t) for t in (1, 2, 3)]
    out_other = swap(out_weight, "core")

    attended = attend(queries, cache_key, cache_value, new_key, new_value, lengths)
    count = attended.shape[0]
    slots = attended.reshape(count, 4, 4, -1).transpose(2, 0, 1, 3).reshape(4, count, -1)
    block = exchange(slots, "z").reshape(4 * count, -1)
    block = jnp.concatenate([block, swap(block, "l")], axis=0)
    block, *out_own[1:] = lax.optimization_barrier((block, *out_own[1:]))
    out_others = swap(jnp.concatenate(out_own[1:], axis=0), "core")
    pieces = [spread(block, step) for step in range(4)]
    partial = project(place, pieces, out_own, out_other, out_others)
    *partial, gate_late, up_late = lax.optimization_barrier((*partial, w_gate, w_up))
    gate_other, up_other = swap(gate_late, "core"), swap(up_late, "core")

    share = hidden_in.shape[0] // 32
    own_in = lax.dynamic_slice_in_dim(hidden_in, (device & 31) * share, share, 0)
    own_in = own_in.reshape(4, 2, count, -1).transpose(1, 0, 2, 3).reshape(share, -1)
    mixed = own_in.astype(jnp.float32) + add_up([partial[0]] + [ring_to(partial[t], "z", t) for t in (1, 2, 3)])
    normed = (mixed * norm_gain).astype(jnp.bfloat16)
    normed, gate_other, up_other = lax.optimization_barrier((normed, gate_other, up_other))

    block = jnp.concatenate([normed] + [ring_from(normed, "z", t) for t in (1, 2, 3)], axis=0)
    block, late = lax.optimization_barrier((block, w_down))
    down_other = swap(late, "core")
    pieces = [block] + [ring_from(block, "y", t) for t in (1, 2, 3)]
    weights = [w_gate, w_up, gate_other, up_other]
    summed = [scatter_sum(gate_up(norm_gain[None, :], part, weights), GRP) for part in (pieces[:2], pieces[2:])]
    summed = jnp.concatenate(summed, axis=0)
    width = w_gate.shape[1]
    square_sum = summed[:, 4 * width] + summed[:, 4 * width + 1]
    hidden = jnp.concatenate(
        [
            activate(summed[:, i * width : (i + 1) * width], summed[:, (i + 1) * width : (i + 2) * width], square_sum)
            for i in (0, 2)
        ],
        axis=1,
    )
    parts = down(gather(hidden, GRP), [w_down, down_other])
    total = add_up([parts[0]] + [ring_to(parts[t], "y", t) for t in (1, 2, 3)])
    parts = [total[t * share : (t + 1) * share] for t in range(4)]
    total = add_up([parts[0]] + [ring_to(parts[t].astype(jnp.bfloat16), "z", t) for t in (1, 2, 3)])
    layer_out = (mixed + total).astype(jnp.bfloat16)
    return layer_out.reshape(2, 4, count, -1).transpose(1, 0, 2, 3).reshape(share, -1)


def solution(mesh):
    fine = Mesh(mesh.devices.reshape(SIZES), NAMES)
    rows = P(GRP + ATT)
    in_specs = (
        P(None, GRP),
        rows,
        rows,
        rows,
        rows,
        rows,
        rows,
        P(ATT, GRP),
        P(GRP),
        P(GRP, ATT),
        P(GRP, ATT),
        P(ATT, GRP),
    )
    out_specs = P(ATT, GRP)
    return jax.shard_map(body, mesh=fine, in_specs=in_specs, out_specs=out_specs, check_vma=False)
```

```python
import jax
import jax.numpy as jnp
import numpy as np
from jax import lax
from jax.experimental import pallas as pl
from jax.experimental.pallas import tpu as pltpu
from jax.sharding import Mesh
from jax.sharding import PartitionSpec as P

NAMES = ("x", "l", "y", "z", "core")
SIZES = (4, 2, 4, 4, 2)
GRP, ATT = ("x", "l"), ("y", "z", "core")
VMEM = pl.BlockSpec(memory_space=pltpu.VMEM)
SMEM = pl.BlockSpec(memory_space=pltpu.SMEM)
ANY = pl.BlockSpec(memory_space=pl.ANY)
STEP = 256

D = 8192
HQ = 64
KVH = 8
HD = 128


def attend(queries, cache_key, cache_value, new_key, new_value, lengths):
    row_count = queries.shape[0]
    slot_count = cache_key.shape[1]
    scale_factor = 1.0 / jnp.sqrt(jnp.float32(HD))
    query_heads = queries.reshape(row_count, KVH, HQ // KVH, HD)
    key_heads = cache_key.reshape(row_count, slot_count, KVH, HD)
    value_heads = cache_value.reshape(row_count, slot_count, KVH, HD)
    scores = (
        jnp.einsum("rkgd,rpkd->rkgp", query_heads, key_heads, preferred_element_type=jnp.float32)
        * scale_factor
    )
    score_new = (
        jnp.einsum(
            "rkgd,rkd->rkg",
            query_heads,
            new_key.reshape(row_count, KVH, HD),
            preferred_element_type=jnp.float32,
        )
        * scale_factor
    )
    valid = jnp.arange(slot_count, dtype=jnp.int32)[None, :] < lengths[:, None]
    scores = jnp.where(valid[:, None, None, :], scores, -jnp.inf)
    top_score = jnp.maximum(jnp.max(scores, axis=-1), score_new)
    weights = jnp.exp(scores - top_score[..., None])
    weight_new = jnp.exp(score_new - top_score)
    total = jnp.sum(weights, axis=-1) + weight_new
    summed = jnp.einsum(
        "rkgp,rpkd->rkgd",
        weights.astype(jnp.bfloat16),
        value_heads,
        preferred_element_type=jnp.float32,
    )
    new_low = weight_new.astype(jnp.bfloat16).astype(jnp.float32)
    summed = summed + new_low[..., None] * new_value.astype(jnp.float32).reshape(
        row_count, KVH, 1, HD
    )
    return (summed / total[..., None]).astype(jnp.bfloat16).reshape(row_count, HQ * HD)


def activate(gate_sum, up_sum, square_sum):
    inv_rms = lax.rsqrt(square_sum / D + 1e-05)
    gate = gate_sum * inv_rms[:, None]
    up_proj = up_sum * inv_rms[:, None]
    return (jax.nn.silu(gate) * up_proj).astype(jnp.bfloat16)


def places():
    table = np.zeros((256, 29), np.int32)
    for device in range(256):
        x, l, y, z, core = device >> 6, (device >> 5) & 1, (device >> 3) & 3, (device >> 1) & 3, device & 1
        owners = [(z + t) % 4 for t in range(4)]
        table[device, :8] = [((x + t) % 4) * 2 + (l ^ b) for t in range(4) for b in range(2)]
        table[device, 8:12] = [(y + t) % 4 for t in range(4)]
        table[device, 12] = core
        table[device, 13:17] = [(y + t - z) % 4 for t in range(4)]
        table[device, 17:25] = [(2 * (owner % 2) + source - y) % 4 for owner in owners for source in range(2)]
        table[device, 25:29] = [owner // 2 for owner in owners]
    return table


def swap(block, axis):
    return lax.ppermute(block, axis, [(0, 1), (1, 0)])


def ring_from(block, axis, shift):
    return lax.ppermute(block, axis, [((i + shift) % 4, i) for i in range(4)])


def ring_to(block, axis, shift):
    return lax.ppermute(block, axis, [(i, (i + shift) % 4) for i in range(4)])


def by_owner_core(block, other):
    perm = []
    for l in range(2):
        for y in range(4):
            for core in range(2):
                target = (((l ^ other) * 4 + (y // 2) * 2 + core) * 2) + y % 2
                perm.append(((l * 4 + y) * 2 + core, target))
    return lax.ppermute(block, ("l", "y", "core"), perm)


def params(mebibytes, flops, nbytes):
    return dict(
        compiler_params=pltpu.CompilerParams(vmem_limit_bytes=mebibytes << 20),
        cost_estimate=pl.CostEstimate(flops=flops, bytes_accessed=nbytes, transcendentals=0),
    )


def steps(width):
    return [(n, min(STEP, width - n)) for n in range(0, width, STEP)]


def start_all(copies):
    for copy in copies:
        copy.start()
    return copies


def wait_all(copies):
    for copy in copies:
        copy.wait()


def project_kernel(place_ref, *refs):
    pieces, own, other, others = refs[:4], refs[4:8], refs[8], refs[9]
    out_ref, rows_ref, held_ref, row_sems, held_sems = refs[10:]
    step = pieces[0].shape[0] // 2
    row_copies = start_all(
        [
            pltpu.make_async_copy(
                pieces[j].at[pl.ds(b * step, step), :],
                rows_ref.at[pl.ds(pl.multiple_of(place_ref[2 * j + b] * step, step), step), :],
                row_sems.at[2 * j + b],
            )
            for j in range(4)
            for b in range(2)
        ]
    )
    depth, width = own[0].shape
    held_copies = []
    for t in range(4):
        for b in range(2):
            source = own[t] if b == 0 else (other if t == 0 else others.at[pl.ds((t - 1) * depth, depth), :])
            start = (2 * place_ref[8 + t] + (place_ref[12] if b == 0 else 1 - place_ref[12])) * depth
            held = held_ref.at[pl.ds(pl.multiple_of(start, depth), depth), :]
            held_copies.append(pltpu.make_async_copy(source, held, held_sems.at[2 * t + b]))
    start_all(held_copies)
    wait_all(row_copies)
    wait_all(held_copies)
    for n, size in steps(width):
        out_ref[:, n : n + size] = jnp.dot(
            rows_ref[...], held_ref[:, n : n + size], preferred_element_type=jnp.float32
        ).astype(out_ref.dtype)


def project(place, pieces, own, other, others):
    count, depth = 4 * pieces[0].shape[0], pieces[0].shape[1]
    width = other.shape[1]
    return pl.pallas_call(
        project_kernel,
        in_specs=[SMEM] + [ANY] * 10,
        out_specs=VMEM,
        out_shape=jax.ShapeDtypeStruct((count, width), jnp.bfloat16),
        scratch_shapes=[
            pltpu.VMEM((count, depth), jnp.bfloat16),
            pltpu.VMEM((depth, width), jnp.bfloat16),
            pltpu.SemaphoreType.DMA((8,)),
            pltpu.SemaphoreType.DMA((8,)),
        ],
        name="project",
        **params(12, 2 * count * depth * width, 2 * (depth * width + count * (depth + width))),
    )(place, *pieces, *own, other, others)


def gate_up_kernel(gain_ref, *refs):
    pieces, weights = refs[:-9], refs[-9:-5]
    out_ref, rows_ref, held_ref, row_sems, held_sems = refs[-5:]
    step = pieces[0].shape[0]
    width = weights[0].shape[1]
    row_copies = start_all(
        [
            pltpu.make_async_copy(piece, rows_ref.at[pl.ds(t * step, step), :], row_sems.at[t])
            for t, piece in enumerate(pieces)
        ]
    )
    held_copies = start_all(
        [pltpu.make_async_copy(weights[j], held_ref.at[j], held_sems.at[j]) for j in range(4)]
    )
    inverse = 1.0 / gain_ref[...]
    part = 64
    lane = lax.broadcasted_iota(jnp.int32, (part, 128), 1)
    wait_all(row_copies)
    for t in range(0, rows_ref.shape[0], part):
        mixed = rows_ref[t : t + part, :].astype(jnp.float32) * inverse
        squares = jnp.sum(mixed * mixed, axis=1, keepdims=True)
        high = squares.astype(jnp.bfloat16).astype(jnp.float32)
        columns = jnp.where(lane == 0, high, jnp.where(lane == 1, squares - high, 0.0))
        out_ref[t : t + part, 4 * width :] = columns.astype(out_ref.dtype)
    for j in range(4):
        held_copies[j].wait()
        for n, size in steps(width):
            product = jnp.dot(rows_ref[...], held_ref[j, :, n : n + size], preferred_element_type=jnp.float32)
            out_ref[:, j * width + n : j * width + n + size] = product.astype(out_ref.dtype)


def gate_up(gain, pieces, weights):
    count, depth = len(pieces) * pieces[0].shape[0], pieces[0].shape[1]
    width = weights[0].shape[1]
    return pl.pallas_call(
        gate_up_kernel,
        in_specs=[VMEM] + [ANY] * (len(pieces) + 4),
        out_specs=VMEM,
        out_shape=jax.ShapeDtypeStruct((count, 4 * width + 128), jnp.bfloat16),
        scratch_shapes=[
            pltpu.VMEM((count, depth), jnp.bfloat16),
            pltpu.VMEM((4, depth, width), jnp.bfloat16),
            pltpu.SemaphoreType.DMA((len(pieces),)),
            pltpu.SemaphoreType.DMA((4,)),
        ],
        name="gate_up",
        **params(20, 8 * count * depth * width, 2 * (count * depth + 4 * depth * width + 4 * count * width)),
    )(gain, *pieces, *weights)


def down_kernel(place_ref, hidden_ref, own, other, mixed_ref, *refs):
    outs, rows_ref, held_ref, total_ref, row_sem, held_sems = refs[:4], *refs[4:]
    depth, width = own.shape
    row_copy = pltpu.make_async_copy(hidden_ref, rows_ref, row_sem.at[0])
    row_copy.start()
    held_copies = start_all(
        [
            pltpu.make_async_copy(weight, held_ref.at[pl.ds(i * depth, depth), :], held_sems.at[i])
            for i, weight in enumerate((own, other))
        ]
    )
    row_copy.wait()
    share = mixed_ref.shape[0]
    first = hidden_ref.shape[1] // 4
    near = rows_ref[:, :first].reshape(4 * share, 2 * depth)
    far = rows_ref[:, first:].reshape(12 * share, 2 * depth)
    wait_all(held_copies)
    for n, size in steps(width):
        columns = held_ref[:, n : n + size]
        product = jnp.dot(near, columns, preferred_element_type=jnp.float32)
        total_ref[:4, :, n : n + size] = product.reshape(4, share, size)
        product = jnp.dot(far, columns, preferred_element_type=jnp.float32)
        total_ref[4:, :, n : n + size] = product.reshape(12, share, size)
    total_ref[0] += mixed_ref[...]
    half = share // 2
    for t in range(4):
        for u in range(4):
            inner = pl.ds(pl.multiple_of(place_ref[25 + u] * half, half), half)
            for source in range(2):
                holder = place_ref[17 + 2 * u + source] * 4 + place_ref[13 + t]
                start = (2 * u + source) * half
                outs[t][start : start + half, :] = total_ref[holder, inner, :].astype(outs[t].dtype)


def down(place, hidden, weights, mixed):
    count = hidden.shape[0] * hidden.shape[1]
    depth, width = weights[0].shape
    return pl.pallas_call(
        down_kernel,
        in_specs=[SMEM] + [ANY] * 3 + [VMEM],
        out_specs=[VMEM] * 4,
        out_shape=[jax.ShapeDtypeStruct((count // 4, width), jnp.bfloat16)] * 4,
        scratch_shapes=[
            pltpu.VMEM(hidden.shape, jnp.bfloat16),
            pltpu.VMEM((2 * depth, width), jnp.bfloat16),
            pltpu.VMEM((16, count // 16, width), jnp.float32),
            pltpu.SemaphoreType.DMA((1,)),
            pltpu.SemaphoreType.DMA((2,)),
        ],
        name="down",
        **params(18, 4 * count * depth * width, 2 * (2 * count * depth + 2 * depth * width + count * width)),
    )(place, hidden, *weights, mixed)


def add_up(pieces):
    total = pieces[0].astype(jnp.float32)
    for piece in pieces[1:]:
        total = total + piece.astype(jnp.float32)
    return total


def exchange(pieces, axis):
    return lax.all_to_all(pieces, axis, split_axis=0, concat_axis=0, tiled=True)


def scatter_sum(partial, axis):
    parts = lax.axis_size(axis)
    pieces = partial.reshape(parts, partial.shape[0] // parts, partial.shape[1])
    return jnp.sum(exchange(pieces, axis).astype(jnp.float32), axis=0)


def gather(rows, axis):
    return exchange(jnp.broadcast_to(rows[None], (lax.axis_size(axis),) + rows.shape), axis)


def body(
    hidden_in,
    queries,
    cache_key,
    cache_value,
    new_key,
    new_value,
    lengths,
    out_weight,
    norm_gain,
    w_gate,
    w_up,
    w_down,
):
    device = lax.axis_index(GRP + ATT)
    place = lax.dynamic_slice_in_dim(jnp.asarray(places()), device, 1, 0)[0]
    out_own = [out_weight] + [ring_from(out_weight, "y", t) for t in (1, 2, 3)]
    out_other = swap(out_weight, "core")

    attended = attend(queries, cache_key, cache_value, new_key, new_value, lengths)
    count = attended.shape[0]
    slots = jnp.stack([by_owner_core(attended, other) for other in range(2)])
    slots = slots.reshape(2, count, 4, 4, -1).transpose(3, 0, 1, 2, 4).reshape(4, 2 * count, -1)
    block = exchange(slots, "z").reshape(4, 2, count, -1).transpose(1, 0, 2, 3).reshape(8 * count, -1)
    block, *out_own[1:] = lax.optimization_barrier((block, *out_own[1:]))
    out_others = swap(jnp.concatenate(out_own[1:], axis=0), "core")
    pieces = [block] + [ring_from(block, "x", t) for t in (1, 2, 3)]
    partial = project(place, pieces, out_own, out_other, out_others)
    partial, *late = lax.optimization_barrier((partial, w_gate, w_up))
    gate_other, up_other = [swap(w, "core") for w in late]

    share = hidden_in.shape[0] // 32
    y, z, core = (device >> 3) & 3, (device >> 1) & 3, device & 1
    start = 256 * z + 32 * (2 * (y >> 1) + core)
    own_in = jnp.stack([lax.dynamic_slice_in_dim(hidden_in, start + 128 * l, share, 0) for l in range(2)])
    own_in = lax.dynamic_index_in_dim(own_in.reshape(2, 4, 2, count, -1), y & 1, 2, keepdims=False).reshape(share, -1)
    mixed = own_in.astype(jnp.float32) + scatter_sum(partial, "z")
    normed = (mixed * norm_gain).astype(jnp.bfloat16)
    normed, gate_other, up_other = lax.optimization_barrier((normed, gate_other, up_other))

    block = jnp.concatenate([normed] + [ring_from(normed, "z", t) for t in (1, 2, 3)], axis=0)
    block, late = lax.optimization_barrier((block, w_down))
    down_other = swap(late, "core")
    pieces = [ring_from(block, "y", t) for t in (1, 2, 3)]
    weights = [w_gate, w_up, gate_other, up_other]
    summed = [scatter_sum(gate_up(norm_gain[None, :], part, weights), GRP) for part in ([block], pieces)]
    summed = jnp.concatenate(summed, axis=0)
    width = w_gate.shape[1]
    square_sum = summed[:, 4 * width] + summed[:, 4 * width + 1]
    hidden = jnp.concatenate(
        [
            activate(summed[:, i * width : (i + 1) * width], summed[:, (i + 1) * width : (i + 2) * width], square_sum)
            for i in (0, 2)
        ],
        axis=1,
    )
    parts = down(place, gather(hidden, GRP), [w_down, down_other], mixed)
    total = add_up([parts[0]] + [ring_to(parts[t], "y", t) for t in (1, 2, 3)])
    parts = [total[t * share : (t + 1) * share] for t in range(4)]
    total = add_up([parts[0]] + [ring_to(parts[t].astype(jnp.bfloat16), "z", t) for t in (1, 2, 3)])
    return total.astype(jnp.bfloat16).reshape(2, 4, count, -1).transpose(1, 0, 2, 3).reshape(share, -1)


def solution(mesh):
    fine = Mesh(mesh.devices.reshape(SIZES), NAMES)
    rows = P(GRP + ATT)
    in_specs = (
        P(None, GRP),
        rows,
        rows,
        rows,
        rows,
        rows,
        rows,
        P(ATT, GRP),
        P(GRP),
        P(GRP, ATT),
        P(GRP, ATT),
        P(ATT, GRP),
    )
    out_specs = P(ATT, GRP)
    return jax.shard_map(body, mesh=fine, in_specs=in_specs, out_specs=out_specs, check_vma=False)
```

```python
import jax
import jax.numpy as jnp
import numpy as np
from jax import lax
from jax.experimental import pallas as pl
from jax.experimental.pallas import tpu as pltpu
from jax.sharding import Mesh
from jax.sharding import PartitionSpec as P

NAMES = ("x", "l", "y", "z", "core")
SIZES = (4, 2, 4, 4, 2)
GRP, ATT = ("x", "l"), ("y", "z", "core")
VMEM = pl.BlockSpec(memory_space=pltpu.VMEM)
SMEM = pl.BlockSpec(memory_space=pltpu.SMEM)
ANY = pl.BlockSpec(memory_space=pl.ANY)
STEP = 256

D = 8192
HQ = 64
KVH = 8
HD = 128


def attend(queries, cache_key, cache_value, new_key, new_value, lengths):
    row_count = queries.shape[0]
    slot_count = cache_key.shape[1]
    scale_factor = 1.0 / jnp.sqrt(jnp.float32(HD))
    query_heads = queries.reshape(row_count, KVH, HQ // KVH, HD)
    key_heads = cache_key.reshape(row_count, slot_count, KVH, HD)
    value_heads = cache_value.reshape(row_count, slot_count, KVH, HD)
    scores = (
        jnp.einsum("rkgd,rpkd->rkgp", query_heads, key_heads, preferred_element_type=jnp.float32)
        * scale_factor
    )
    score_new = (
        jnp.einsum(
            "rkgd,rkd->rkg",
            query_heads,
            new_key.reshape(row_count, KVH, HD),
            preferred_element_type=jnp.float32,
        )
        * scale_factor
    )
    valid = jnp.arange(slot_count, dtype=jnp.int32)[None, :] < lengths[:, None]
    scores = jnp.where(valid[:, None, None, :], scores, -jnp.inf)
    top_score = jnp.maximum(jnp.max(scores, axis=-1), score_new)
    weights = jnp.exp(scores - top_score[..., None])
    weight_new = jnp.exp(score_new - top_score)
    total = jnp.sum(weights, axis=-1) + weight_new
    summed = jnp.einsum(
        "rkgp,rpkd->rkgd",
        weights.astype(jnp.bfloat16),
        value_heads,
        preferred_element_type=jnp.float32,
    )
    new_low = weight_new.astype(jnp.bfloat16).astype(jnp.float32)
    summed = summed + new_low[..., None] * new_value.astype(jnp.float32).reshape(
        row_count, KVH, 1, HD
    )
    return (summed / total[..., None]).astype(jnp.bfloat16).reshape(row_count, HQ * HD)


def activate(gate_sum, up_sum, square_sum):
    inv_rms = lax.rsqrt(square_sum / D + 1e-05)
    gate = gate_sum * inv_rms[:, None]
    up_proj = up_sum * inv_rms[:, None]
    return (jax.nn.silu(gate) * up_proj).astype(jnp.bfloat16)


def places():
    table = np.zeros((256, 29), np.int32)
    for device in range(256):
        x, l, y, z, core = device >> 6, (device >> 5) & 1, (device >> 3) & 3, (device >> 1) & 3, device & 1
        owners = [(z + t) % 4 for t in range(4)]
        table[device, :8] = [((x + t) % 4) * 2 + (l ^ b) for t in range(4) for b in range(2)]
        table[device, 8:12] = [(y + t) % 4 for t in range(4)]
        table[device, 12] = core
        table[device, 13:17] = [(y + t - z) % 4 for t in range(4)]
        table[device, 17:25] = [(2 * (owner % 2) + source - y) % 4 for owner in owners for source in range(2)]
        table[device, 25:29] = [owner // 2 for owner in owners]
    return table


def swap(block, axis):
    return lax.ppermute(block, axis, [(0, 1), (1, 0)])


def ring_from(block, axis, shift):
    return lax.ppermute(block, axis, [((i + shift) % 4, i) for i in range(4)])


def ring_to(block, axis, shift):
    return lax.ppermute(block, axis, [(i, (i + shift) % 4) for i in range(4)])


def params(mebibytes, flops, nbytes):
    return dict(
        compiler_params=pltpu.CompilerParams(vmem_limit_bytes=mebibytes << 20),
        cost_estimate=pl.CostEstimate(flops=flops, bytes_accessed=nbytes, transcendentals=0),
    )


def steps(width):
    return [(n, min(STEP, width - n)) for n in range(0, width, STEP)]


def start_all(copies):
    for copy in copies:
        copy.start()
    return copies


def wait_all(copies):
    for copy in copies:
        copy.wait()


def project_kernel(place_ref, *refs):
    pieces, own, other = refs[:4], refs[4:8], refs[8:12]
    out_ref, rows_ref, held_ref, row_sems, held_sems = refs[12:]
    step = pieces[0].shape[0] // 2
    row_copies = start_all(
        [
            pltpu.make_async_copy(
                pieces[j].at[pl.ds(b * step, step), :],
                rows_ref.at[pl.ds(pl.multiple_of(place_ref[2 * j + b] * step, step), step), :],
                row_sems.at[2 * j + b],
            )
            for j in range(4)
            for b in range(2)
        ]
    )
    depth, width = own[0].shape
    held_copies = []
    for t in range(4):
        for b in range(2):
            source = own[t] if b == 0 else other[t]
            start = (2 * place_ref[8 + t] + (place_ref[12] if b == 0 else 1 - place_ref[12])) * depth
            held = held_ref.at[pl.ds(pl.multiple_of(start, depth), depth), :]
            held_copies.append(pltpu.make_async_copy(source, held, held_sems.at[2 * t + b]))
    start_all(held_copies)
    wait_all(row_copies)
    wait_all(held_copies)
    for n, size in steps(width):
        out_ref[:, n : n + size] = jnp.dot(
            rows_ref[...], held_ref[:, n : n + size], preferred_element_type=jnp.float32
        ).astype(out_ref.dtype)


def project(place, pieces, own, other):
    count, depth = 4 * pieces[0].shape[0], pieces[0].shape[1]
    width = own[0].shape[1]
    return pl.pallas_call(
        project_kernel,
        in_specs=[SMEM] + [ANY] * 12,
        out_specs=VMEM,
        out_shape=jax.ShapeDtypeStruct((count, width), jnp.bfloat16),
        scratch_shapes=[
            pltpu.VMEM((count, depth), jnp.bfloat16),
            pltpu.VMEM((depth, width), jnp.bfloat16),
            pltpu.SemaphoreType.DMA((8,)),
            pltpu.SemaphoreType.DMA((8,)),
        ],
        name="project",
        **params(12, 2 * count * depth * width, 2 * (depth * width + count * (depth + width))),
    )(place, *pieces, *own, *other)


def gate_up_kernel(gain_ref, *refs):
    pieces, weights = refs[:-9], refs[-9:-5]
    out_ref, rows_ref, held_ref, row_sems, held_sems = refs[-5:]
    step = pieces[0].shape[0]
    width = weights[0].shape[1]
    row_copies = start_all(
        [
            pltpu.make_async_copy(piece, rows_ref.at[pl.ds(t * step, step), :], row_sems.at[t])
            for t, piece in enumerate(pieces)
        ]
    )
    held_copies = start_all(
        [pltpu.make_async_copy(weights[j], held_ref.at[j], held_sems.at[j]) for j in range(4)]
    )
    inverse = 1.0 / gain_ref[...]
    part = 64
    lane = lax.broadcasted_iota(jnp.int32, (part, 128), 1)
    wait_all(row_copies)
    for t in range(0, rows_ref.shape[0], part):
        mixed = rows_ref[t : t + part, :].astype(jnp.float32) * inverse
        squares = jnp.sum(mixed * mixed, axis=1, keepdims=True)
        high = squares.astype(jnp.bfloat16).astype(jnp.float32)
        columns = jnp.where(lane == 0, high, jnp.where(lane == 1, squares - high, 0.0))
        out_ref[t : t + part, 4 * width :] = columns.astype(out_ref.dtype)
    for j in range(4):
        held_copies[j].wait()
        for n, size in steps(width):
            product = jnp.dot(rows_ref[...], held_ref[j, :, n : n + size], preferred_element_type=jnp.float32)
            out_ref[:, j * width + n : j * width + n + size] = product.astype(out_ref.dtype)


def gate_up(gain, pieces, weights):
    count, depth = len(pieces) * pieces[0].shape[0], pieces[0].shape[1]
    width = weights[0].shape[1]
    return pl.pallas_call(
        gate_up_kernel,
        in_specs=[VMEM] + [ANY] * (len(pieces) + 4),
        out_specs=VMEM,
        out_shape=jax.ShapeDtypeStruct((count, 4 * width + 128), jnp.bfloat16),
        scratch_shapes=[
            pltpu.VMEM((count, depth), jnp.bfloat16),
            pltpu.VMEM((4, depth, width), jnp.bfloat16),
            pltpu.SemaphoreType.DMA((len(pieces),)),
            pltpu.SemaphoreType.DMA((4,)),
        ],
        name="gate_up",
        **params(20, 8 * count * depth * width, 2 * (count * depth + 4 * depth * width + 4 * count * width)),
    )(gain, *pieces, *weights)


def down_kernel(place_ref, hidden_ref, own, other, mixed_ref, *refs):
    outs, rows_ref, held_ref, total_ref, row_sem, held_sems = refs[:4], *refs[4:]
    depth, width = own.shape
    row_copy = pltpu.make_async_copy(hidden_ref, rows_ref, row_sem.at[0])
    row_copy.start()
    held_copies = start_all(
        [
            pltpu.make_async_copy(weight, held_ref.at[pl.ds(i * depth, depth), :], held_sems.at[i])
            for i, weight in enumerate((own, other))
        ]
    )
    row_copy.wait()
    share = mixed_ref.shape[0]
    first = hidden_ref.shape[1] // 4
    near = rows_ref[:, :first].reshape(4 * share, 2 * depth)
    far = rows_ref[:, first:].reshape(12 * share, 2 * depth)
    wait_all(held_copies)
    for n, size in steps(width):
        columns = held_ref[:, n : n + size]
        product = jnp.dot(near, columns, preferred_element_type=jnp.float32)
        total_ref[:4, :, n : n + size] = product.reshape(4, share, size)
        product = jnp.dot(far, columns, preferred_element_type=jnp.float32)
        total_ref[4:, :, n : n + size] = product.reshape(12, share, size)
    total_ref[0] += mixed_ref[...]
    half = share // 2
    for t in range(4):
        for u in range(4):
            inner = pl.ds(pl.multiple_of(place_ref[25 + u] * half, half), half)
            for source in range(2):
                holder = place_ref[17 + 2 * u + source] * 4 + place_ref[13 + t]
                start = (2 * u + source) * half
                outs[t][start : start + half, :] = total_ref[holder, inner, :].astype(outs[t].dtype)


def down(place, hidden, weights, mixed):
    count = hidden.shape[0] * hidden.shape[1]
    depth, width = weights[0].shape
    return pl.pallas_call(
        down_kernel,
        in_specs=[SMEM] + [ANY] * 3 + [VMEM],
        out_specs=[VMEM] * 4,
        out_shape=[jax.ShapeDtypeStruct((count // 4, width), jnp.bfloat16)] * 4,
        scratch_shapes=[
            pltpu.VMEM(hidden.shape, jnp.bfloat16),
            pltpu.VMEM((2 * depth, width), jnp.bfloat16),
            pltpu.VMEM((16, count // 16, width), jnp.float32),
            pltpu.SemaphoreType.DMA((1,)),
            pltpu.SemaphoreType.DMA((2,)),
        ],
        name="down",
        **params(18, 4 * count * depth * width, 2 * (2 * count * depth + 2 * depth * width + count * width)),
    )(place, hidden, *weights, mixed)


def add_up(pieces):
    total = pieces[0].astype(jnp.float32)
    for piece in pieces[1:]:
        total = total + piece.astype(jnp.float32)
    return total


def exchange(pieces, axis):
    return lax.all_to_all(pieces, axis, split_axis=0, concat_axis=0, tiled=True)


def scatter_sum(partial, axis):
    parts = lax.axis_size(axis)
    pieces = partial.reshape(parts, partial.shape[0] // parts, partial.shape[1])
    return jnp.sum(exchange(pieces, axis).astype(jnp.float32), axis=0)


def gather(rows, axis):
    return exchange(jnp.broadcast_to(rows[None], (lax.axis_size(axis),) + rows.shape), axis)


def body(
    hidden_in,
    queries,
    cache_key,
    cache_value,
    new_key,
    new_value,
    lengths,
    out_weight,
    norm_gain,
    w_gate,
    w_up,
    w_down,
):
    device = lax.axis_index(GRP + ATT)
    place = lax.dynamic_slice_in_dim(jnp.asarray(places()), device, 1, 0)[0]
    out_own = [out_weight] + [ring_from(out_weight, "y", t) for t in (1, 2, 3)]
    out_other = swap(out_weight, "core")

    attended = attend(queries, cache_key, cache_value, new_key, new_value, lengths)
    count = attended.shape[0]
    slots = attended.reshape(count, 4, 4, -1).transpose(2, 0, 1, 3).reshape(4, count, -1)
    block = exchange(slots, "z").reshape(4 * count, -1)
    block, out_own[1], out_own[3] = lax.optimization_barrier((block, out_own[1], out_own[3]))
    out_next, out_last = swap(out_own[1], "core"), swap(out_own[3], "core")
    block = jnp.concatenate([block, swap(block, "l")], axis=0)
    pieces = [block] + [ring_from(block, "x", t) for t in (1, 2, 3)]
    *pieces, out_own[2] = lax.optimization_barrier((*pieces, out_own[2]))
    partial = project(place, pieces, out_own, [out_other, out_next, swap(out_own[2], "core"), out_last])
    partial, *late = lax.optimization_barrier((partial, w_gate, w_up))
    gate_other, up_other = [swap(w, "core") for w in late]

    share = hidden_in.shape[0] // 32
    y, z, core = (device >> 3) & 3, (device >> 1) & 3, device & 1
    start = 256 * z + 32 * y
    own_in = jnp.stack([lax.dynamic_slice_in_dim(hidden_in, start + 128 * l, share, 0) for l in range(2)])
    own_in = lax.dynamic_index_in_dim(own_in.reshape(2, 4, 2, count, -1), core, 2, keepdims=False).reshape(share, -1)
    mixed = own_in.astype(jnp.float32) + scatter_sum(partial, "z")
    normed = (mixed * norm_gain).astype(jnp.bfloat16)
    normed, gate_other, up_other = lax.optimization_barrier((normed, gate_other, up_other))

    block = jnp.concatenate([normed] + [ring_from(normed, "z", t) for t in (1, 2, 3)], axis=0)
    block, late = lax.optimization_barrier((block, w_down))
    down_other = swap(late, "core")
    pieces = [ring_from(block, "y", t) for t in (1, 2, 3)]
    weights = [w_gate, w_up, gate_other, up_other]
    summed = [scatter_sum(gate_up(norm_gain[None, :], part, weights), GRP) for part in ([block], pieces)]
    summed = jnp.concatenate(summed, axis=0)
    width = w_gate.shape[1]
    square_sum = summed[:, 4 * width] + summed[:, 4 * width + 1]
    hidden = jnp.concatenate(
        [
            activate(summed[:, i * width : (i + 1) * width], summed[:, (i + 1) * width : (i + 2) * width], square_sum)
            for i in (0, 2)
        ],
        axis=1,
    )
    parts = down(place, gather(hidden, GRP), [w_down, down_other], mixed)
    total = add_up([parts[0]] + [ring_to(parts[t], "y", t) for t in (1, 2, 3)])
    parts = [total[t * share : (t + 1) * share] for t in range(4)]
    total = add_up([parts[0]] + [ring_to(parts[t].astype(jnp.bfloat16), "z", t) for t in (1, 2, 3)])
    total = total.astype(jnp.bfloat16)
    half = share // 2
    low, high = total[:half], total[half:]
    given = swap(jnp.where(core == 0, high, low), "core")
    rows = jnp.stack([jnp.where(core == 0, low, given), jnp.where(core == 0, given, high)])
    return rows.reshape(2, 4, count, -1).transpose(1, 0, 2, 3).reshape(share, -1)


def solution(mesh):
    fine = Mesh(mesh.devices.reshape(SIZES), NAMES)
    rows = P(GRP + ATT)
    in_specs = (
        P(None, GRP),
        rows,
        rows,
        rows,
        rows,
        rows,
        rows,
        P(ATT, GRP),
        P(GRP),
        P(GRP, ATT),
        P(GRP, ATT),
        P(ATT, GRP),
    )
    out_specs = P(ATT, GRP)
    return jax.shard_map(body, mesh=fine, in_specs=in_specs, out_specs=out_specs, check_vma=False)
```

```python
import jax
import jax.numpy as jnp
import numpy as np
from jax import lax
from jax.experimental import pallas as pl
from jax.experimental.pallas import tpu as pltpu
from jax.sharding import Mesh
from jax.sharding import PartitionSpec as P

NAMES = ("x", "l", "y", "z", "core")
SIZES = (4, 2, 4, 4, 2)
GRP, ATT = ("x", "l"), ("y", "z", "core")
VMEM = pl.BlockSpec(memory_space=pltpu.VMEM)
SMEM = pl.BlockSpec(memory_space=pltpu.SMEM)
ANY = pl.BlockSpec(memory_space=pl.ANY)
STEP = 256

D = 8192
HQ = 64
KVH = 8
HD = 128


def attend(queries, cache_key, cache_value, new_key, new_value, lengths):
    row_count = queries.shape[0]
    slot_count = cache_key.shape[1]
    scale_factor = 1.0 / jnp.sqrt(jnp.float32(HD))
    query_heads = queries.reshape(row_count, KVH, HQ // KVH, HD)
    key_heads = cache_key.reshape(row_count, slot_count, KVH, HD)
    value_heads = cache_value.reshape(row_count, slot_count, KVH, HD)
    scores = (
        jnp.einsum("rkgd,rpkd->rkgp", query_heads, key_heads, preferred_element_type=jnp.float32)
        * scale_factor
    )
    score_new = (
        jnp.einsum(
            "rkgd,rkd->rkg",
            query_heads,
            new_key.reshape(row_count, KVH, HD),
            preferred_element_type=jnp.float32,
        )
        * scale_factor
    )
    valid = jnp.arange(slot_count, dtype=jnp.int32)[None, :] < lengths[:, None]
    scores = jnp.where(valid[:, None, None, :], scores, -jnp.inf)
    top_score = jnp.maximum(jnp.max(scores, axis=-1), score_new)
    weights = jnp.exp(scores - top_score[..., None])
    weight_new = jnp.exp(score_new - top_score)
    total = jnp.sum(weights, axis=-1) + weight_new
    summed = jnp.einsum(
        "rkgp,rpkd->rkgd",
        weights.astype(jnp.bfloat16),
        value_heads,
        preferred_element_type=jnp.float32,
    )
    new_low = weight_new.astype(jnp.bfloat16).astype(jnp.float32)
    summed = summed + new_low[..., None] * new_value.astype(jnp.float32).reshape(
        row_count, KVH, 1, HD
    )
    return (summed / total[..., None]).astype(jnp.bfloat16).reshape(row_count, HQ * HD)


def activate(gate_sum, up_sum, square_sum):
    inv_rms = lax.rsqrt(square_sum / D + 1e-05)
    gate = gate_sum * inv_rms[:, None]
    up_proj = up_sum * inv_rms[:, None]
    return (jax.nn.silu(gate) * up_proj).astype(jnp.bfloat16)


def places():
    table = np.zeros((256, 29), np.int32)
    for device in range(256):
        x, l, y, z, core = device >> 6, (device >> 5) & 1, (device >> 3) & 3, (device >> 1) & 3, device & 1
        owners = [(z + t) % 4 for t in range(4)]
        table[device, :8] = [((x + t) % 4) * 2 + (l ^ b) for t in range(4) for b in range(2)]
        table[device, 8:12] = [(y + t) % 4 for t in range(4)]
        table[device, 12] = core
        table[device, 13:17] = [(y + t - z) % 4 for t in range(4)]
        table[device, 17:25] = [(2 * (owner % 2) + source - y) % 4 for owner in owners for source in range(2)]
        table[device, 25:29] = [owner // 2 for owner in owners]
    return table


def swap(block, axis):
    return lax.ppermute(block, axis, [(0, 1), (1, 0)])


def ring_from(block, axis, shift):
    return lax.ppermute(block, axis, [((i + shift) % 4, i) for i in range(4)])


def ring_to(block, axis, shift):
    return lax.ppermute(block, axis, [(i, (i + shift) % 4) for i in range(4)])


def params(mebibytes, flops, nbytes):
    return dict(
        compiler_params=pltpu.CompilerParams(vmem_limit_bytes=mebibytes << 20),
        cost_estimate=pl.CostEstimate(flops=flops, bytes_accessed=nbytes, transcendentals=0),
    )


def steps(width):
    return [(n, min(STEP, width - n)) for n in range(0, width, STEP)]


def start_all(copies):
    for copy in copies:
        copy.start()
    return copies


def wait_all(copies):
    for copy in copies:
        copy.wait()


def project_kernel(place_ref, *refs):
    pieces, own, other = refs[:4], refs[4:8], refs[8:12]
    out_ref, rows_ref, held_ref, row_sems, held_sems = refs[12:]
    step = pieces[0].shape[0] // 2
    row_copies = start_all(
        [
            pltpu.make_async_copy(
                pieces[j].at[pl.ds(b * step, step), :],
                rows_ref.at[pl.ds(pl.multiple_of(place_ref[2 * j + b] * step, step), step), :],
                row_sems.at[2 * j + b],
            )
            for j in range(4)
            for b in range(2)
        ]
    )
    depth, width = own[0].shape
    held_copies = []
    for t in range(4):
        for b in range(2):
            source = own[t] if b == 0 else other[t]
            start = (2 * place_ref[8 + t] + (place_ref[12] if b == 0 else 1 - place_ref[12])) * depth
            held = held_ref.at[pl.ds(pl.multiple_of(start, depth), depth), :]
            held_copies.append(pltpu.make_async_copy(source, held, held_sems.at[2 * t + b]))
    start_all(held_copies)
    wait_all(row_copies)
    wait_all(held_copies)
    for n, size in steps(width):
        out_ref[:, n : n + size] = jnp.dot(
            rows_ref[...], held_ref[:, n : n + size], preferred_element_type=jnp.float32
        ).astype(out_ref.dtype)


def project(place, pieces, own, other):
    count, depth = 4 * pieces[0].shape[0], pieces[0].shape[1]
    width = own[0].shape[1]
    return pl.pallas_call(
        project_kernel,
        in_specs=[SMEM] + [ANY] * 12,
        out_specs=VMEM,
        out_shape=jax.ShapeDtypeStruct((count, width), jnp.bfloat16),
        scratch_shapes=[
            pltpu.VMEM((count, depth), jnp.bfloat16),
            pltpu.VMEM((depth, width), jnp.bfloat16),
            pltpu.SemaphoreType.DMA((8,)),
            pltpu.SemaphoreType.DMA((8,)),
        ],
        name="project",
        **params(12, 2 * count * depth * width, 2 * (depth * width + count * (depth + width))),
    )(place, *pieces, *own, *other)


def gate_up_kernel(gain_ref, *refs):
    pieces, weights = refs[:-9], refs[-9:-5]
    out_ref, rows_ref, held_ref, row_sems, held_sems = refs[-5:]
    step = pieces[0].shape[0]
    width = weights[0].shape[1]
    row_copies = start_all(
        [
            pltpu.make_async_copy(piece, rows_ref.at[pl.ds(t * step, step), :], row_sems.at[t])
            for t, piece in enumerate(pieces)
        ]
    )
    held_copies = start_all(
        [pltpu.make_async_copy(weights[j], held_ref.at[j], held_sems.at[j]) for j in range(4)]
    )
    inverse = 1.0 / gain_ref[...]
    part = 64
    lane = lax.broadcasted_iota(jnp.int32, (part, 128), 1)
    wait_all(row_copies)
    for t in range(0, rows_ref.shape[0], part):
        mixed = rows_ref[t : t + part, :].astype(jnp.float32) * inverse
        squares = jnp.sum(mixed * mixed, axis=1, keepdims=True)
        high = squares.astype(jnp.bfloat16).astype(jnp.float32)
        columns = jnp.where(lane == 0, high, jnp.where(lane == 1, squares - high, 0.0))
        out_ref[t : t + part, 4 * width :] = columns.astype(out_ref.dtype)
    for j in range(4):
        held_copies[j].wait()
        for n, size in steps(width):
            product = jnp.dot(rows_ref[...], held_ref[j, :, n : n + size], preferred_element_type=jnp.float32)
            out_ref[:, j * width + n : j * width + n + size] = product.astype(out_ref.dtype)


def gate_up(gain, pieces, weights, hidden_us):
    count, depth = len(pieces) * pieces[0].shape[0], pieces[0].shape[1]
    width = weights[0].shape[1]
    return pl.pallas_call(
        gate_up_kernel,
        in_specs=[VMEM] + [ANY] * (len(pieces) + 4),
        out_specs=VMEM,
        out_shape=jax.ShapeDtypeStruct((count, 4 * width + 128), jnp.bfloat16),
        scratch_shapes=[
            pltpu.VMEM((count, depth), jnp.bfloat16),
            pltpu.VMEM((4, depth, width), jnp.bfloat16),
            pltpu.SemaphoreType.DMA((len(pieces),)),
            pltpu.SemaphoreType.DMA((4,)),
        ],
        name="gate_up",
        **params(20, hidden_us * 1153500000, 2 * (count * depth + 4 * depth * width + 4 * count * width)),
    )(gain, *pieces, *weights)


def down_kernel(place_ref, hidden_ref, own, other, mixed_ref, *refs):
    outs, rows_ref, held_ref, total_ref, row_sem, held_sems = refs[:4], *refs[4:]
    depth, width = own.shape
    row_copy = pltpu.make_async_copy(hidden_ref, rows_ref, row_sem.at[0])
    row_copy.start()
    held_copies = start_all(
        [
            pltpu.make_async_copy(weight, held_ref.at[pl.ds(i * depth, depth), :], held_sems.at[i])
            for i, weight in enumerate((own, other))
        ]
    )
    row_copy.wait()
    share = mixed_ref.shape[0]
    first = hidden_ref.shape[1] // 4
    near = rows_ref[:, :first].reshape(4 * share, 2 * depth)
    far = rows_ref[:, first:].reshape(12 * share, 2 * depth)
    wait_all(held_copies)
    for n, size in steps(width):
        columns = held_ref[:, n : n + size]
        product = jnp.dot(near, columns, preferred_element_type=jnp.float32)
        total_ref[:4, :, n : n + size] = product.reshape(4, share, size)
        product = jnp.dot(far, columns, preferred_element_type=jnp.float32)
        total_ref[4:, :, n : n + size] = product.reshape(12, share, size)
    total_ref[0] += mixed_ref[...]
    half = share // 2
    for t in range(4):
        for u in range(4):
            inner = pl.ds(pl.multiple_of(place_ref[25 + u] * half, half), half)
            for source in range(2):
                holder = place_ref[17 + 2 * u + source] * 4 + place_ref[13 + t]
                start = (2 * u + source) * half
                outs[t][start : start + half, :] = total_ref[holder, inner, :].astype(outs[t].dtype)


def down(place, hidden, weights, mixed):
    count = hidden.shape[0] * hidden.shape[1]
    depth, width = weights[0].shape
    return pl.pallas_call(
        down_kernel,
        in_specs=[SMEM] + [ANY] * 3 + [VMEM],
        out_specs=[VMEM] * 4,
        out_shape=[jax.ShapeDtypeStruct((count // 4, width), jnp.bfloat16)] * 4,
        scratch_shapes=[
            pltpu.VMEM(hidden.shape, jnp.bfloat16),
            pltpu.VMEM((2 * depth, width), jnp.bfloat16),
            pltpu.VMEM((16, count // 16, width), jnp.float32),
            pltpu.SemaphoreType.DMA((1,)),
            pltpu.SemaphoreType.DMA((2,)),
        ],
        name="down",
        **params(60, 4 * count * depth * width, 2 * (2 * count * depth + 2 * depth * width + count * width)),
    )(place, hidden, *weights, mixed)


def add_up(pieces):
    total = pieces[0].astype(jnp.float32)
    for piece in pieces[1:]:
        total = total + piece.astype(jnp.float32)
    return total


def exchange(pieces, axis):
    return lax.all_to_all(pieces, axis, split_axis=0, concat_axis=0, tiled=True)


def scatter_sum(partial, axis):
    parts = lax.axis_size(axis)
    pieces = partial.reshape(parts, partial.shape[0] // parts, partial.shape[1])
    return jnp.sum(exchange(pieces, axis).astype(jnp.float32), axis=0)


def gather(rows, axis):
    return exchange(jnp.broadcast_to(rows[None], (lax.axis_size(axis),) + rows.shape), axis)


def body(
    hidden_in,
    queries,
    cache_key,
    cache_value,
    new_key,
    new_value,
    lengths,
    out_weight,
    norm_gain,
    w_gate,
    w_up,
    w_down,
):
    device = lax.axis_index(GRP + ATT)
    place = lax.dynamic_slice_in_dim(jnp.asarray(places()), device, 1, 0)[0]
    out_own = [out_weight] + [ring_from(out_weight, "y", t) for t in (1, 2, 3)]
    out_other = swap(out_weight, "core")

    attended = attend(queries, cache_key, cache_value, new_key, new_value, lengths)
    count = attended.shape[0]
    slots = attended.reshape(count, 4, 4, -1).transpose(2, 0, 1, 3).reshape(4, count, -1)
    block = exchange(slots, "z").reshape(4 * count, -1)
    block, out_own[1], out_own[3] = lax.optimization_barrier((block, out_own[1], out_own[3]))
    out_next, out_last = swap(out_own[1], "core"), swap(out_own[3], "core")
    block = jnp.concatenate([block, swap(block, "l")], axis=0)
    pieces = [block] + [ring_from(block, "x", t) for t in (1, 2, 3)]
    *pieces, out_own[2] = lax.optimization_barrier((*pieces, out_own[2]))
    partial = project(place, pieces, out_own, [out_other, out_next, swap(out_own[2], "core"), out_last])
    partial, *late = lax.optimization_barrier((partial, w_gate, w_up))
    gate_other, up_other = [swap(w, "core") for w in late]

    share = hidden_in.shape[0] // 32
    y, z, core = (device >> 3) & 3, (device >> 1) & 3, device & 1
    start = 256 * z + 32 * y
    own_in = jnp.stack([lax.dynamic_slice_in_dim(hidden_in, start + 128 * l, share, 0) for l in range(2)])
    own_in = lax.dynamic_index_in_dim(own_in.reshape(2, 4, 2, count, -1), core, 2, keepdims=False).reshape(share, -1)
    mixed = own_in.astype(jnp.float32) + scatter_sum(partial, "z")
    normed = (mixed * norm_gain).astype(jnp.bfloat16)
    normed, gate_other, up_other = lax.optimization_barrier((normed, gate_other, up_other))

    block = jnp.concatenate([normed] + [ring_from(normed, "z", t) for t in (1, 2, 3)], axis=0)
    block, late = lax.optimization_barrier((block, w_down))
    down_other = swap(late, "core")
    pieces = [ring_from(block, "y", t) for t in (1, 2, 3)]
    weights = [w_gate, w_up, gate_other, up_other]
    summed = [
        scatter_sum(gate_up(norm_gain[None, :], part, weights, hidden_us), GRP)
        for part, hidden_us in (([block], 15), (pieces, 60))
    ]
    summed = jnp.concatenate(summed, axis=0)
    width = w_gate.shape[1]
    square_sum = summed[:, 4 * width] + summed[:, 4 * width + 1]
    hidden = jnp.concatenate(
        [
            activate(summed[:, i * width : (i + 1) * width], summed[:, (i + 1) * width : (i + 2) * width], square_sum)
            for i in (0, 2)
        ],
        axis=1,
    )
    parts = down(place, gather(hidden, GRP), [w_down, down_other], mixed)
    total = add_up([parts[0]] + [ring_to(parts[t], "y", t) for t in (1, 2, 3)])
    parts = [total[t * share : (t + 1) * share] for t in range(4)]
    total = add_up([parts[0]] + [ring_to(parts[t].astype(jnp.bfloat16), "z", t) for t in (1, 2, 3)])
    total = total.astype(jnp.bfloat16)
    half = share // 2
    low, high = total[:half], total[half:]
    given = swap(jnp.where(core == 0, high, low), "core")
    rows = jnp.stack([jnp.where(core == 0, low, given), jnp.where(core == 0, given, high)])
    return rows.reshape(2, 4, count, -1).transpose(1, 0, 2, 3).reshape(share, -1)


def solution(mesh):
    fine = Mesh(mesh.devices.reshape(SIZES), NAMES)
    rows = P(GRP + ATT)
    in_specs = (
        P(None, GRP),
        rows,
        rows,
        rows,
        rows,
        rows,
        rows,
        P(ATT, GRP),
        P(GRP),
        P(GRP, ATT),
        P(GRP, ATT),
        P(ATT, GRP),
    )
    out_specs = P(ATT, GRP)
    return jax.shard_map(body, mesh=fine, in_specs=in_specs, out_specs=out_specs, check_vma=False)
```

```python
import jax
import jax.numpy as jnp
import numpy as np
from jax import lax
from jax.experimental import pallas as pl
from jax.experimental.pallas import tpu as pltpu
from jax.sharding import Mesh
from jax.sharding import PartitionSpec as P

NAMES = ("x", "l", "y", "z", "core")
SIZES = (4, 2, 4, 4, 2)
GRP, ATT = ("x", "l"), ("y", "z", "core")
BLOCK = pl.BlockSpec()
VMEM = pl.BlockSpec(memory_space=pltpu.VMEM)
SMEM = pl.BlockSpec(memory_space=pltpu.SMEM)
ANY = pl.BlockSpec(memory_space=pl.ANY)
STEP = 256

D = 8192
HQ = 64
KVH = 8
HD = 128


def places():
    table = np.zeros((256, 33), np.int32)
    for device in range(256):
        x, l, y, z, core = device >> 6, (device >> 5) & 1, (device >> 3) & 3, (device >> 1) & 3, device & 1
        owners = [(z + t) % 4 for t in range(4)]
        table[device, :8] = [((x + t) % 4) * 2 + (l ^ b) for t in range(4) for b in range(2)]
        table[device, 8:12] = [(y + t) % 4 for t in range(4)]
        table[device, 12] = core
        table[device, 13:17] = [(y + t - z) % 4 for t in range(4)]
        table[device, 17:25] = [(2 * (owner % 2) + source - y) % 4 for owner in owners for source in range(2)]
        table[device, 25:29] = [owner // 2 for owner in owners]
        table[device, 29:] = owners
    return table


def swap(block, axis):
    return lax.ppermute(block, axis, [(0, 1), (1, 0)])


def ring_from(block, axis, shift):
    return lax.ppermute(block, axis, [((i + shift) % 4, i) for i in range(4)])


def ring_to(block, axis, shift):
    return lax.ppermute(block, axis, [(i, (i + shift) % 4) for i in range(4)])


def params(mebibytes, flops, nbytes):
    return dict(
        compiler_params=pltpu.CompilerParams(vmem_limit_bytes=mebibytes << 20),
        cost_estimate=pl.CostEstimate(flops=flops, bytes_accessed=nbytes, transcendentals=0),
    )


def steps(width):
    return [(n, min(STEP, width - n)) for n in range(0, width, STEP)]


def start_all(copies):
    for copy in copies:
        copy.start()
    return copies


def wait_all(copies):
    for copy in copies:
        copy.wait()


def attend_kernel(lengths_ref, queries_ref, new_key_ref, new_value_ref, keys, values, out_ref):
    rows, slot_count = keys.shape[:2]
    group = HQ // KVH
    scale_factor = 1.0 / jnp.sqrt(jnp.float32(HD))
    slot = lax.broadcasted_iota(jnp.int32, (HQ, slot_count), 1)
    for r in range(rows):

        def per_head(ref):
            spread = jnp.broadcast_to(ref[r].astype(jnp.float32)[:, None, :], (KVH, group, HD))
            return spread.reshape(HQ, HD)

        query = queries_ref[r]
        scores = [
            lax.dot_general(
                query[k * group : (k + 1) * group],
                keys[r, :, k * HD : (k + 1) * HD],
                (((1,), (1,)), ((), ())),
                preferred_element_type=jnp.float32,
            )
            for k in range(KVH)
        ]
        scores = jnp.where(slot < lengths_ref[r], jnp.concatenate(scores, axis=0) * scale_factor, -jnp.inf)
        products = query.astype(jnp.float32) * per_head(new_key_ref)
        score_new = jnp.sum(products, axis=1, keepdims=True) * scale_factor
        top_score = jnp.maximum(jnp.max(scores, axis=1, keepdims=True), score_new)
        weights = jnp.exp(scores - top_score)
        weight_new = jnp.exp(score_new - top_score)
        total = jnp.sum(weights, axis=1, keepdims=True) + weight_new
        weights = weights.astype(jnp.bfloat16)
        summed = [
            jnp.dot(
                weights[k * group : (k + 1) * group],
                values[r, :, k * HD : (k + 1) * HD],
                preferred_element_type=jnp.float32,
            )
            for k in range(KVH)
        ]
        new_low = weight_new.astype(jnp.bfloat16).astype(jnp.float32)
        summed = jnp.concatenate(summed, axis=0) + new_low * per_head(new_value_ref)
        out_ref[r] = (summed / total).astype(out_ref.dtype)


def attend(queries, cache_key, cache_value, new_key, new_value, lengths):
    rows, slot_count, width = cache_key.shape
    return pl.pallas_call(
        attend_kernel,
        in_specs=[SMEM] + [VMEM] * 5,
        out_specs=BLOCK,
        out_shape=jax.ShapeDtypeStruct((rows, HQ, HD), jnp.bfloat16),
        name="attend",
        **params(12, 4 * rows * slot_count * HQ * HD, 4 * rows * slot_count * width),
    )(
        lengths,
        queries.reshape(rows, HQ, HD),
        new_key.reshape(rows, KVH, HD),
        new_value.reshape(rows, KVH, HD),
        cache_key,
        cache_value,
    )


def activate_kernel(*refs):
    parts, out_ref, held, hidden_ref, sems = refs[:2], refs[2], refs[3:5], refs[5], refs[6]
    copies = start_all([pltpu.make_async_copy(parts[i], held[i], sems.at[i]) for i in range(2)])
    width = hidden_ref.shape[1] // 2
    start = 0
    for i in range(2):
        copies[i].wait()
        groups, rows = held[i].shape[:2]

        def summed(first, size):
            return add_up([held[i][g, :, first : first + size] for g in range(groups)])

        square_sum = jnp.sum(summed(4 * width, 128), axis=1, keepdims=True)
        inv_rms = lax.rsqrt(square_sum / D + 1e-05)
        for j in range(2):
            for n, size in steps(width):
                gate = summed(2 * j * width + n, size) * inv_rms
                up_proj = summed((2 * j + 1) * width + n, size) * inv_rms
                hidden = gate / (1.0 + jnp.exp(-gate)) * up_proj
                hidden_ref[start : start + rows, j * width + n : j * width + n + size] = hidden.astype(jnp.bfloat16)
        start += rows
    wait_all(
        start_all(
            [pltpu.make_async_copy(hidden_ref, out_ref.at[g], sems.at[2 + g]) for g in range(out_ref.shape[0])]
        )
    )


def activate(parts):
    groups, _, width = parts[0].shape
    width = (width - 128) // 2
    rows = parts[0].shape[1] + parts[1].shape[1]
    return pl.pallas_call(
        activate_kernel,
        in_specs=[ANY] * 2,
        out_specs=ANY,
        out_shape=jax.ShapeDtypeStruct((groups, rows, width), jnp.bfloat16),
        scratch_shapes=[pltpu.VMEM(part.shape, jnp.bfloat16) for part in parts]
        + [pltpu.VMEM((rows, width), jnp.bfloat16), pltpu.SemaphoreType.DMA((2 + groups,))],
        name="activate",
        **params(12, 0, 6 * groups * rows * width),
    )(*parts)


def project_kernel(place_ref, *refs):
    pieces, own, other = refs[:4], refs[4:8], refs[8:12]
    outs, (rows_ref, held_ref, total_ref, row_sems, held_sems) = refs[12:16], refs[16:]
    step = pieces[0].shape[0] // 2
    row_copies = start_all(
        [
            pltpu.make_async_copy(
                pieces[j].at[pl.ds(b * step, step), :],
                rows_ref.at[pl.ds(pl.multiple_of(place_ref[2 * j + b] * step, step), step), :],
                row_sems.at[2 * j + b],
            )
            for j in range(4)
            for b in range(2)
        ]
    )
    depth, width = own[0].shape
    held_copies = []
    for t in range(4):
        for b in range(2):
            source = own[t] if b == 0 else other[t]
            start = (2 * place_ref[8 + t] + (place_ref[12] if b == 0 else 1 - place_ref[12])) * depth
            held = held_ref.at[pl.ds(pl.multiple_of(start, depth), depth), :]
            held_copies.append(pltpu.make_async_copy(source, held, held_sems.at[2 * t + b]))
    start_all(held_copies)
    wait_all(row_copies)
    wait_all(held_copies)
    for n, size in steps(width):
        total_ref[:, n : n + size] = jnp.dot(
            rows_ref[...], held_ref[:, n : n + size], preferred_element_type=jnp.float32
        )
    share = outs[0].shape[0]
    for t in range(4):
        start = pl.multiple_of(place_ref[29 + t] * share, share)
        outs[t][...] = total_ref[pl.ds(start, share), :].astype(outs[t].dtype)


def project(place, pieces, own, other):
    count, depth = 4 * pieces[0].shape[0], pieces[0].shape[1]
    width = own[0].shape[1]
    return pl.pallas_call(
        project_kernel,
        in_specs=[SMEM] + [ANY] * 12,
        out_specs=[VMEM] * 4,
        out_shape=[jax.ShapeDtypeStruct((count // 4, width), jnp.bfloat16)] * 4,
        scratch_shapes=[
            pltpu.VMEM((count, depth), jnp.bfloat16),
            pltpu.VMEM((depth, width), jnp.bfloat16),
            pltpu.VMEM((count, width), jnp.float32),
            pltpu.SemaphoreType.DMA((8,)),
            pltpu.SemaphoreType.DMA((8,)),
        ],
        name="project",
        **params(12, 2 * count * depth * width, 2 * (depth * width + count * (depth + width))),
    )(place, *pieces, *own, *other)


def gate_up_kernel(gain_ref, *refs):
    pieces, weights = refs[:-9], refs[-9:-5]
    out_ref, rows_ref, held_ref, row_sems, held_sems = refs[-5:]
    step = pieces[0].shape[0]
    width = weights[0].shape[1]
    row_copies = start_all(
        [
            pltpu.make_async_copy(piece, rows_ref.at[pl.ds(t * step, step), :], row_sems.at[t])
            for t, piece in enumerate(pieces)
        ]
    )
    held_copies = start_all(
        [pltpu.make_async_copy(weights[j], held_ref.at[j], held_sems.at[j]) for j in range(4)]
    )
    inverse = 1.0 / gain_ref[...]
    part = 64
    lane = lax.broadcasted_iota(jnp.int32, (part, 128), 1)
    wait_all(row_copies)
    for t in range(0, rows_ref.shape[0], part):
        mixed = rows_ref[t : t + part, :].astype(jnp.float32) * inverse
        squares = jnp.sum(mixed * mixed, axis=1, keepdims=True)
        high = squares.astype(jnp.bfloat16).astype(jnp.float32)
        columns = jnp.where(lane == 0, high, jnp.where(lane == 1, squares - high, 0.0))
        out_ref[t : t + part, 4 * width :] = columns.astype(out_ref.dtype)
    for j in range(4):
        held_copies[j].wait()
        for n, size in steps(width):
            product = jnp.dot(rows_ref[...], held_ref[j, :, n : n + size], preferred_element_type=jnp.float32)
            out_ref[:, j * width + n : j * width + n + size] = product.astype(out_ref.dtype)


def gate_up(gain, pieces, weights, hidden_us):
    count, depth = len(pieces) * pieces[0].shape[0], pieces[0].shape[1]
    width = weights[0].shape[1]
    return pl.pallas_call(
        gate_up_kernel,
        in_specs=[VMEM] + [ANY] * (len(pieces) + 4),
        out_specs=VMEM,
        out_shape=jax.ShapeDtypeStruct((count, 4 * width + 128), jnp.bfloat16),
        scratch_shapes=[
            pltpu.VMEM((count, depth), jnp.bfloat16),
            pltpu.VMEM((4, depth, width), jnp.bfloat16),
            pltpu.SemaphoreType.DMA((len(pieces),)),
            pltpu.SemaphoreType.DMA((4,)),
        ],
        name="gate_up",
        **params(20, hidden_us * 1153500000, 2 * (count * depth + 4 * depth * width + 4 * count * width)),
    )(gain, *pieces, *weights)


def down_kernel(place_ref, hidden_ref, own, other, mixed_ref, *refs):
    outs, rows_ref, held_ref, total_ref, row_sem, held_sems = refs[:4], *refs[4:]
    depth, width = own.shape
    row_copy = pltpu.make_async_copy(hidden_ref, rows_ref, row_sem.at[0])
    row_copy.start()
    held_copies = start_all(
        [
            pltpu.make_async_copy(weight, held_ref.at[pl.ds(i * depth, depth), :], held_sems.at[i])
            for i, weight in enumerate((own, other))
        ]
    )
    row_copy.wait()
    share = mixed_ref.shape[0]
    first = hidden_ref.shape[1] // 4
    near = rows_ref[:, :first].reshape(4 * share, 2 * depth)
    far = rows_ref[:, first:].reshape(12 * share, 2 * depth)
    wait_all(held_copies)
    for n, size in steps(width):
        columns = held_ref[:, n : n + size]
        product = jnp.dot(near, columns, preferred_element_type=jnp.float32)
        total_ref[:4, :, n : n + size] = product.reshape(4, share, size)
        product = jnp.dot(far, columns, preferred_element_type=jnp.float32)
        total_ref[4:, :, n : n + size] = product.reshape(12, share, size)
    total_ref[0] += mixed_ref[...]
    half = share // 2
    for t in range(4):
        for u in range(4):
            inner = pl.ds(pl.multiple_of(place_ref[25 + u] * half, half), half)
            for source in range(2):
                holder = place_ref[17 + 2 * u + source] * 4 + place_ref[13 + t]
                start = (2 * u + source) * half
                outs[t][start : start + half, :] = total_ref[holder, inner, :].astype(outs[t].dtype)


def down(place, hidden, weights, mixed):
    count = hidden.shape[0] * hidden.shape[1]
    depth, width = weights[0].shape
    return pl.pallas_call(
        down_kernel,
        in_specs=[SMEM] + [ANY] * 3 + [VMEM],
        out_specs=[VMEM] * 4,
        out_shape=[jax.ShapeDtypeStruct((count // 4, width), jnp.bfloat16)] * 4,
        scratch_shapes=[
            pltpu.VMEM(hidden.shape, jnp.bfloat16),
            pltpu.VMEM((2 * depth, width), jnp.bfloat16),
            pltpu.VMEM((16, count // 16, width), jnp.float32),
            pltpu.SemaphoreType.DMA((1,)),
            pltpu.SemaphoreType.DMA((2,)),
        ],
        name="down",
        **params(60, 4 * count * depth * width, 2 * (2 * count * depth + 2 * depth * width + count * width)),
    )(place, hidden, *weights, mixed)


def add_up(pieces):
    total = pieces[0].astype(jnp.float32)
    for piece in pieces[1:]:
        total = total + piece.astype(jnp.float32)
    return total


def exchange(pieces, axis):
    return lax.all_to_all(pieces, axis, split_axis=0, concat_axis=0, tiled=True)


def body(
    hidden_in,
    queries,
    cache_key,
    cache_value,
    new_key,
    new_value,
    lengths,
    out_weight,
    norm_gain,
    w_gate,
    w_up,
    w_down,
):
    device = lax.axis_index(GRP + ATT)
    place = lax.dynamic_slice_in_dim(jnp.asarray(places()), device, 1, 0)[0]
    out_own = [out_weight] + [ring_from(out_weight, "y", t) for t in (1, 2, 3)]
    out_other = swap(out_weight, "core")

    attended = attend(queries, cache_key, cache_value, new_key, new_value, lengths)
    count = queries.shape[0]
    slots = attended.reshape(count, 4, 4, -1).transpose(2, 0, 1, 3).reshape(4, count, -1)
    block = exchange(slots, "z").reshape(4 * count, -1)
    block, out_own[1], out_own[3] = lax.optimization_barrier((block, out_own[1], out_own[3]))
    out_next, out_last = swap(out_own[1], "core"), swap(out_own[3], "core")
    block = jnp.concatenate([block, swap(block, "l")], axis=0)
    pieces = [block] + [ring_from(block, "x", t) for t in (1, 2, 3)]
    *pieces, out_own[2] = lax.optimization_barrier((*pieces, out_own[2]))
    partial = project(place, pieces, out_own, [out_other, out_next, swap(out_own[2], "core"), out_last])

    share = hidden_in.shape[0] // 32
    y, z, core = (device >> 3) & 3, (device >> 1) & 3, device & 1
    start = 256 * z + 32 * y
    own_in = jnp.stack([lax.dynamic_slice_in_dim(hidden_in, start + 128 * l, share, 0) for l in range(2)])
    own_in = lax.dynamic_index_in_dim(own_in.reshape(2, 4, 2, count, -1), core, 2, keepdims=False).reshape(share, -1)
    mixed = own_in.astype(jnp.float32) + add_up([partial[0]] + [ring_to(partial[t], "z", t) for t in (1, 2, 3)])
    normed = (mixed * norm_gain).astype(jnp.bfloat16)
    normed, *late = lax.optimization_barrier((normed, w_gate, w_up))
    gate_other, up_other = [swap(w, "core") for w in late]

    block = jnp.concatenate([normed] + [ring_from(normed, "z", t) for t in (1, 2, 3)], axis=0)
    block, late = lax.optimization_barrier((block, w_down))
    down_other = swap(late, "core")
    pieces = [ring_from(block, "y", t) for t in (1, 2, 3)]
    weights = [w_gate, w_up, gate_other, up_other]
    summed = [
        exchange(gate_up(norm_gain[None, :], part, weights, hidden_us).reshape(8, -1, 4 * w_gate.shape[1] + 128), GRP)
        for part, hidden_us in (([block], 15), (pieces, 60))
    ]
    hidden = exchange(activate(summed), GRP)
    parts = down(place, hidden, [w_down, down_other], mixed)
    total = add_up([parts[0]] + [ring_to(parts[t], "y", t) for t in (1, 2, 3)])
    parts = [total[t * share : (t + 1) * share] for t in range(4)]
    total = add_up([parts[0]] + [ring_to(parts[t].astype(jnp.bfloat16), "z", t) for t in (1, 2, 3)])
    total = total.astype(jnp.bfloat16)
    half = share // 2
    low, high = total[:half], total[half:]
    given = swap(jnp.where(core == 0, high, low), "core")
    rows = jnp.stack([jnp.where(core == 0, low, given), jnp.where(core == 0, given, high)])
    return rows.reshape(2, 4, count, -1).transpose(1, 0, 2, 3).reshape(share, -1)


def solution(mesh):
    fine = Mesh(mesh.devices.reshape(SIZES), NAMES)
    rows = P(GRP + ATT)
    in_specs = (
        P(None, GRP),
        rows,
        rows,
        rows,
        rows,
        rows,
        rows,
        P(ATT, GRP),
        P(GRP),
        P(GRP, ATT),
        P(GRP, ATT),
        P(ATT, GRP),
    )
    out_specs = P(ATT, GRP)
    return jax.shard_map(body, mesh=fine, in_specs=in_specs, out_specs=out_specs, check_vma=False)
```

```python
import jax
import jax.numpy as jnp
import numpy as np
from jax import lax
from jax.experimental import pallas as pl
from jax.experimental.pallas import tpu as pltpu
from jax.sharding import Mesh
from jax.sharding import PartitionSpec as P

NAMES = ("x", "l", "y", "z", "core")
SIZES = (4, 2, 4, 4, 2)
GRP, ATT = ("x", "l"), ("y", "z", "core")
BLOCK = pl.BlockSpec()
VMEM = pl.BlockSpec(memory_space=pltpu.VMEM)
SMEM = pl.BlockSpec(memory_space=pltpu.SMEM)
ANY = pl.BlockSpec(memory_space=pl.ANY)
STEP = 256

D = 8192
HQ = 64
KVH = 8
HD = 128


def places():
    table = np.zeros((256, 29), np.int32)
    for device in range(256):
        x, l, y, z, core = device >> 6, (device >> 5) & 1, (device >> 3) & 3, (device >> 1) & 3, device & 1
        owners = [(z + t) % 4 for t in range(4)]
        table[device, :8] = [((x + t) % 4) * 2 + (l ^ b) for t in range(4) for b in range(2)]
        table[device, 8:12] = [(y + t) % 4 for t in range(4)]
        table[device, 12] = core
        table[device, 13:17] = [(y + t - z) % 4 for t in range(4)]
        table[device, 17:25] = [(2 * (owner % 2) + source - y) % 4 for owner in owners for source in range(2)]
        table[device, 25:29] = [owner // 2 for owner in owners]
    return table


def swap(block, axis):
    return lax.ppermute(block, axis, [(0, 1), (1, 0)])


def ring_from(block, axis, shift):
    return lax.ppermute(block, axis, [((i + shift) % 4, i) for i in range(4)])


def ring_to(block, axis, shift):
    return lax.ppermute(block, axis, [(i, (i + shift) % 4) for i in range(4)])


def params(mebibytes, flops, nbytes):
    return dict(
        compiler_params=pltpu.CompilerParams(vmem_limit_bytes=mebibytes << 20),
        cost_estimate=pl.CostEstimate(flops=flops, bytes_accessed=nbytes, transcendentals=0),
    )


def steps(width):
    return [(n, min(STEP, width - n)) for n in range(0, width, STEP)]


def start_all(copies):
    for copy in copies:
        copy.start()
    return copies


def wait_all(copies):
    for copy in copies:
        copy.wait()


def attend_kernel(lengths_ref, queries_ref, new_key_ref, new_value_ref, key_ref, value_ref, out_ref, keys, values, sems):
    rows, slot_count = keys.shape[:2]
    group = HQ // KVH
    copies = start_all(
        [
            pltpu.make_async_copy(source.at[r], held.at[r], sems.at[i, r])
            for r in range(rows)
            for i, (source, held) in enumerate(((key_ref, keys), (value_ref, values)))
        ]
    )
    scale_factor = 1.0 / jnp.sqrt(jnp.float32(HD))
    slot = lax.broadcasted_iota(jnp.int32, (HQ, slot_count), 1)
    for r in range(rows):

        def per_head(ref):
            spread = jnp.broadcast_to(ref[r].astype(jnp.float32)[:, None, :], (KVH, group, HD))
            return spread.reshape(HQ, HD)

        query = queries_ref[r]
        copies[2 * r].wait()
        scores = [
            lax.dot_general(
                query[k * group : (k + 1) * group],
                keys[r, :, k * HD : (k + 1) * HD],
                (((1,), (1,)), ((), ())),
                preferred_element_type=jnp.float32,
            )
            for k in range(KVH)
        ]
        scores = jnp.where(slot < lengths_ref[r], jnp.concatenate(scores, axis=0) * scale_factor, -jnp.inf)
        products = query.astype(jnp.float32) * per_head(new_key_ref)
        score_new = jnp.sum(products, axis=1, keepdims=True) * scale_factor
        top_score = jnp.maximum(jnp.max(scores, axis=1, keepdims=True), score_new)
        weights = jnp.exp(scores - top_score)
        weight_new = jnp.exp(score_new - top_score)
        total = jnp.sum(weights, axis=1, keepdims=True) + weight_new
        weights = weights.astype(jnp.bfloat16)
        copies[2 * r + 1].wait()
        summed = [
            jnp.dot(
                weights[k * group : (k + 1) * group],
                values[r, :, k * HD : (k + 1) * HD],
                preferred_element_type=jnp.float32,
            )
            for k in range(KVH)
        ]
        new_low = weight_new.astype(jnp.bfloat16).astype(jnp.float32)
        summed = jnp.concatenate(summed, axis=0) + new_low * per_head(new_value_ref)
        out_ref[r] = (summed / total).astype(out_ref.dtype)


def attend(queries, cache_key, cache_value, new_key, new_value, lengths):
    rows, slot_count, width = cache_key.shape
    return pl.pallas_call(
        attend_kernel,
        in_specs=[SMEM] + [BLOCK] * 3 + [ANY] * 2,
        out_specs=BLOCK,
        out_shape=jax.ShapeDtypeStruct((rows, HQ, HD), jnp.bfloat16),
        scratch_shapes=[
            pltpu.VMEM((rows, slot_count, width), jnp.bfloat16),
            pltpu.VMEM((rows, slot_count, width), jnp.bfloat16),
            pltpu.SemaphoreType.DMA((2, rows)),
        ],
        name="attend",
        **params(60, 4 * rows * slot_count * HQ * HD, 4 * rows * slot_count * width),
    )(
        lengths,
        queries.reshape(rows, HQ, HD),
        new_key.reshape(rows, KVH, HD),
        new_value.reshape(rows, KVH, HD),
        cache_key,
        cache_value,
    )


def activate_kernel(*refs):
    parts, out_ref, held, hidden_ref, sems = refs[:2], refs[2], refs[3:5], refs[5], refs[6]
    copies = start_all([pltpu.make_async_copy(parts[i], held[i], sems.at[i]) for i in range(2)])
    width = hidden_ref.shape[1] // 2
    start = 0
    for i in range(2):
        copies[i].wait()
        groups, rows = held[i].shape[:2]

        def summed(first, size):
            return add_up([held[i][g, :, first : first + size] for g in range(groups)])

        square_sum = jnp.sum(summed(4 * width, 128), axis=1, keepdims=True)
        inv_rms = lax.rsqrt(square_sum / D + 1e-05)
        for j in range(2):
            for n, size in steps(width):
                gate = summed(2 * j * width + n, size) * inv_rms
                up_proj = summed((2 * j + 1) * width + n, size) * inv_rms
                hidden = gate / (1.0 + jnp.exp(-gate)) * up_proj
                hidden_ref[start : start + rows, j * width + n : j * width + n + size] = hidden.astype(jnp.bfloat16)
        start += rows
    wait_all(
        start_all(
            [pltpu.make_async_copy(hidden_ref, out_ref.at[g], sems.at[2 + g]) for g in range(out_ref.shape[0])]
        )
    )


def activate(parts):
    groups, _, width = parts[0].shape
    width = (width - 128) // 2
    rows = parts[0].shape[1] + parts[1].shape[1]
    return pl.pallas_call(
        activate_kernel,
        in_specs=[ANY] * 2,
        out_specs=ANY,
        out_shape=jax.ShapeDtypeStruct((groups, rows, width), jnp.bfloat16),
        scratch_shapes=[pltpu.VMEM(part.shape, jnp.bfloat16) for part in parts]
        + [pltpu.VMEM((rows, width), jnp.bfloat16), pltpu.SemaphoreType.DMA((2 + groups,))],
        name="activate",
        **params(12, 0, 6 * groups * rows * width),
    )(*parts)


def project_kernel(place_ref, *refs):
    pieces, own, other = refs[:4], refs[4:8], refs[8:12]
    out_ref, rows_ref, held_ref, row_sems, held_sems = refs[12:]
    step = pieces[0].shape[0] // 2
    row_copies = start_all(
        [
            pltpu.make_async_copy(
                pieces[j].at[pl.ds(b * step, step), :],
                rows_ref.at[pl.ds(pl.multiple_of(place_ref[2 * j + b] * step, step), step), :],
                row_sems.at[2 * j + b],
            )
            for j in range(4)
            for b in range(2)
        ]
    )
    depth, width = own[0].shape
    held_copies = []
    for t in range(4):
        for b in range(2):
            source = own[t] if b == 0 else other[t]
            start = (2 * place_ref[8 + t] + (place_ref[12] if b == 0 else 1 - place_ref[12])) * depth
            held_rows = pl.ds(pl.multiple_of(start, depth), depth)
            for i, (n, size) in enumerate(steps(width)):
                cols = pl.ds(n, size)
                held_copies.append(
                    pltpu.make_async_copy(
                        source.at[:, cols], held_ref.at[held_rows, cols], held_sems.at[i, 2 * t + b]
                    )
                )
    blocks = len(steps(width))
    for i in range(blocks):
        start_all(held_copies[i::blocks])
    wait_all(row_copies)
    for i, (n, size) in enumerate(steps(width)):
        wait_all(held_copies[i::blocks])
        out_ref[:, n : n + size] = jnp.dot(
            rows_ref[...], held_ref[:, n : n + size], preferred_element_type=jnp.float32
        ).astype(out_ref.dtype)


def project(place, pieces, own, other):
    count, depth = 4 * pieces[0].shape[0], pieces[0].shape[1]
    width = own[0].shape[1]
    return pl.pallas_call(
        project_kernel,
        in_specs=[SMEM] + [ANY] * 12,
        out_specs=VMEM,
        out_shape=jax.ShapeDtypeStruct((count, width), jnp.bfloat16),
        scratch_shapes=[
            pltpu.VMEM((count, depth), jnp.bfloat16),
            pltpu.VMEM((depth, width), jnp.bfloat16),
            pltpu.SemaphoreType.DMA((8,)),
            pltpu.SemaphoreType.DMA((len(steps(width)), 8)),
        ],
        name="project",
        **params(12, 2 * count * depth * width, 2 * (depth * width + count * (depth + width))),
    )(place, *pieces, *own, *other)


def gate_up_kernel(gain_ref, *refs):
    pieces, weights = refs[:-9], refs[-9:-5]
    out_ref, rows_ref, held_ref, row_sems, held_sems = refs[-5:]
    step = pieces[0].shape[0]
    width = weights[0].shape[1]
    row_copies = start_all(
        [
            pltpu.make_async_copy(piece, rows_ref.at[pl.ds(t * step, step), :], row_sems.at[t])
            for t, piece in enumerate(pieces)
        ]
    )
    held_copies = start_all(
        [pltpu.make_async_copy(weights[j], held_ref.at[j], held_sems.at[j]) for j in range(4)]
    )
    inverse = 1.0 / gain_ref[...]
    part = 64
    lane = lax.broadcasted_iota(jnp.int32, (part, 128), 1)
    wait_all(row_copies)
    for t in range(0, rows_ref.shape[0], part):
        mixed = rows_ref[t : t + part, :].astype(jnp.float32) * inverse
        squares = jnp.sum(mixed * mixed, axis=1, keepdims=True)
        high = squares.astype(jnp.bfloat16).astype(jnp.float32)
        columns = jnp.where(lane == 0, high, jnp.where(lane == 1, squares - high, 0.0))
        out_ref[t : t + part, 4 * width :] = columns.astype(out_ref.dtype)
    for j in range(4):
        held_copies[j].wait()
        for n, size in steps(width):
            product = jnp.dot(rows_ref[...], held_ref[j, :, n : n + size], preferred_element_type=jnp.float32)
            out_ref[:, j * width + n : j * width + n + size] = product.astype(out_ref.dtype)


def gate_up(gain, pieces, weights, hidden_us):
    count, depth = len(pieces) * pieces[0].shape[0], pieces[0].shape[1]
    width = weights[0].shape[1]
    return pl.pallas_call(
        gate_up_kernel,
        in_specs=[VMEM] + [ANY] * (len(pieces) + 4),
        out_specs=VMEM,
        out_shape=jax.ShapeDtypeStruct((count, 4 * width + 128), jnp.bfloat16),
        scratch_shapes=[
            pltpu.VMEM((count, depth), jnp.bfloat16),
            pltpu.VMEM((4, depth, width), jnp.bfloat16),
            pltpu.SemaphoreType.DMA((len(pieces),)),
            pltpu.SemaphoreType.DMA((4,)),
        ],
        name="gate_up",
        **params(20, hidden_us * 1153500000, 2 * (count * depth + 4 * depth * width + 4 * count * width)),
    )(gain, *pieces, *weights)


def down_kernel(place_ref, hidden_ref, own, other, mixed_ref, *refs):
    outs, rows_ref, held_ref, total_ref, row_sem, held_sems = refs[:4], *refs[4:]
    depth, width = own.shape
    row_copy = pltpu.make_async_copy(hidden_ref, rows_ref, row_sem.at[0])
    row_copy.start()
    held_copies = start_all(
        [
            pltpu.make_async_copy(
                weight.at[:, pl.ds(n, size)],
                held_ref.at[pl.ds(i * depth, depth), pl.ds(n, size)],
                held_sems.at[j, i],
            )
            for j, (n, size) in enumerate(steps(width))
            for i, weight in enumerate((own, other))
        ]
    )
    row_copy.wait()
    share = mixed_ref.shape[0]
    first = hidden_ref.shape[1] // 4
    near = rows_ref[:, :first].reshape(4 * share, 2 * depth)
    far = rows_ref[:, first:].reshape(12 * share, 2 * depth)
    for j, (n, size) in enumerate(steps(width)):
        wait_all(held_copies[2 * j : 2 * j + 2])
        columns = held_ref[:, n : n + size]
        product = jnp.dot(near, columns, preferred_element_type=jnp.float32)
        total_ref[:4, :, n : n + size] = product.reshape(4, share, size)
        product = jnp.dot(far, columns, preferred_element_type=jnp.float32)
        total_ref[4:, :, n : n + size] = product.reshape(12, share, size)
    total_ref[0] += mixed_ref[...]
    half = share // 2
    for t in range(4):
        for u in range(4):
            inner = pl.ds(pl.multiple_of(place_ref[25 + u] * half, half), half)
            for source in range(2):
                holder = place_ref[17 + 2 * u + source] * 4 + place_ref[13 + t]
                start = (2 * u + source) * half
                outs[t][start : start + half, :] = total_ref[holder, inner, :].astype(outs[t].dtype)


def down(place, hidden, weights, mixed):
    count = hidden.shape[0] * hidden.shape[1]
    depth, width = weights[0].shape
    return pl.pallas_call(
        down_kernel,
        in_specs=[SMEM] + [ANY] * 3 + [VMEM],
        out_specs=[VMEM] * 4,
        out_shape=[jax.ShapeDtypeStruct((count // 4, width), jnp.bfloat16)] * 4,
        scratch_shapes=[
            pltpu.VMEM(hidden.shape, jnp.bfloat16),
            pltpu.VMEM((2 * depth, width), jnp.bfloat16),
            pltpu.VMEM((16, count // 16, width), jnp.float32),
            pltpu.SemaphoreType.DMA((1,)),
            pltpu.SemaphoreType.DMA((len(steps(width)), 2)),
        ],
        name="down",
        **params(60, 4 * count * depth * width, 2 * (2 * count * depth + 2 * depth * width + count * width)),
    )(place, hidden, *weights, mixed)


def add_up(pieces):
    total = pieces[0].astype(jnp.float32)
    for piece in pieces[1:]:
        total = total + piece.astype(jnp.float32)
    return total


def exchange(pieces, axis):
    return lax.all_to_all(pieces, axis, split_axis=0, concat_axis=0, tiled=True)


def scatter_sum(partial, axis):
    parts = lax.axis_size(axis)
    pieces = partial.reshape(parts, partial.shape[0] // parts, partial.shape[1])
    return jnp.sum(exchange(pieces, axis).astype(jnp.float32), axis=0)


def body(
    hidden_in,
    queries,
    cache_key,
    cache_value,
    new_key,
    new_value,
    lengths,
    out_weight,
    norm_gain,
    w_gate,
    w_up,
    w_down,
):
    device = lax.axis_index(GRP + ATT)
    place = lax.dynamic_slice_in_dim(jnp.asarray(places()), device, 1, 0)[0]
    out_own = [out_weight] + [ring_from(out_weight, "y", t) for t in (1, 2, 3)]
    out_other = swap(out_weight, "core")

    attended = attend(queries, cache_key, cache_value, new_key, new_value, lengths)
    count = queries.shape[0]
    slots = attended.reshape(count, 4, 4, -1).transpose(2, 0, 1, 3).reshape(4, count, -1)
    block = exchange(slots, "z").reshape(4 * count, -1)
    block, out_own[1], out_own[3] = lax.optimization_barrier((block, out_own[1], out_own[3]))
    out_next, out_last = swap(out_own[1], "core"), swap(out_own[3], "core")
    block = jnp.concatenate([block, swap(block, "l")], axis=0)
    pieces = [block] + [ring_from(block, "x", t) for t in (1, 2, 3)]
    *pieces, out_own[2] = lax.optimization_barrier((*pieces, out_own[2]))
    partial = project(place, pieces, out_own, [out_other, out_next, swap(out_own[2], "core"), out_last])
    partial, *late = lax.optimization_barrier((partial, w_gate, w_up))
    gate_other, up_other = [swap(w, "core") for w in late]

    share = hidden_in.shape[0] // 32
    y, z, core = (device >> 3) & 3, (device >> 1) & 3, device & 1
    start = 256 * z + 32 * y
    own_in = jnp.stack([lax.dynamic_slice_in_dim(hidden_in, start + 128 * l, share, 0) for l in range(2)])
    own_in = lax.dynamic_index_in_dim(own_in.reshape(2, 4, 2, count, -1), core, 2, keepdims=False).reshape(share, -1)
    mixed = own_in.astype(jnp.float32) + scatter_sum(partial, "z")
    normed = (mixed * norm_gain).astype(jnp.bfloat16)
    normed, gate_other, up_other = lax.optimization_barrier((normed, gate_other, up_other))

    block = jnp.concatenate([normed] + [ring_from(normed, "z", t) for t in (1, 2, 3)], axis=0)
    block, late = lax.optimization_barrier((block, w_down))
    down_other = swap(late, "core")
    pieces = [ring_from(block, "y", t) for t in (1, 2, 3)]
    weights = [w_gate, w_up, gate_other, up_other]
    summed = [
        exchange(gate_up(norm_gain[None, :], part, weights, hidden_us).reshape(8, -1, 4 * w_gate.shape[1] + 128), GRP)
        for part, hidden_us in (([block], 15), (pieces, 60))
    ]
    hidden = exchange(activate(summed), GRP)
    parts = down(place, hidden, [w_down, down_other], mixed)
    total = add_up([parts[0]] + [ring_to(parts[t], "y", t) for t in (1, 2, 3)])
    parts = [total[t * share : (t + 1) * share] for t in range(4)]
    total = add_up([parts[0]] + [ring_to(parts[t].astype(jnp.bfloat16), "z", t) for t in (1, 2, 3)])
    total = total.astype(jnp.bfloat16)
    half = share // 2
    low, high = total[:half], total[half:]
    given = swap(jnp.where(core == 0, high, low), "core")
    rows = jnp.stack([jnp.where(core == 0, low, given), jnp.where(core == 0, given, high)])
    return rows.reshape(2, 4, count, -1).transpose(1, 0, 2, 3).reshape(share, -1)


def solution(mesh):
    fine = Mesh(mesh.devices.reshape(SIZES), NAMES)
    rows = P(GRP + ATT)
    in_specs = (
        P(None, GRP),
        rows,
        rows,
        rows,
        rows,
        rows,
        rows,
        P(ATT, GRP),
        P(GRP),
        P(GRP, ATT),
        P(GRP, ATT),
        P(ATT, GRP),
    )
    out_specs = P(ATT, GRP)
    return jax.shard_map(body, mesh=fine, in_specs=in_specs, out_specs=out_specs, check_vma=False)
```

```python
import jax
import jax.numpy as jnp
import numpy as np
from jax import lax
from jax.experimental import pallas as pl
from jax.experimental.pallas import tpu as pltpu
from jax.sharding import Mesh
from jax.sharding import PartitionSpec as P

NAMES = ("x", "l", "y", "z", "core")
SIZES = (4, 2, 4, 4, 2)
GRP, ATT = ("x", "l"), ("y", "z", "core")
VMEM = pl.BlockSpec(memory_space=pltpu.VMEM)
SMEM = pl.BlockSpec(memory_space=pltpu.SMEM)
ANY = pl.BlockSpec(memory_space=pl.ANY)
STEP = 256

D = 8192
HQ = 64
KVH = 8
HD = 128


def attend(queries, cache_key, cache_value, new_key, new_value, lengths):
    row_count = queries.shape[0]
    slot_count = cache_key.shape[1]
    scale_factor = 1.0 / jnp.sqrt(jnp.float32(HD))
    query_heads = queries.reshape(row_count, KVH, HQ // KVH, HD)
    key_heads = cache_key.reshape(row_count, slot_count, KVH, HD)
    value_heads = cache_value.reshape(row_count, slot_count, KVH, HD)
    scores = (
        jnp.einsum("rkgd,rpkd->rkgp", query_heads, key_heads, preferred_element_type=jnp.float32)
        * scale_factor
    )
    score_new = (
        jnp.einsum(
            "rkgd,rkd->rkg",
            query_heads,
            new_key.reshape(row_count, KVH, HD),
            preferred_element_type=jnp.float32,
        )
        * scale_factor
    )
    valid = jnp.arange(slot_count, dtype=jnp.int32)[None, :] < lengths[:, None]
    scores = jnp.where(valid[:, None, None, :], scores, -jnp.inf)
    top_score = jnp.maximum(jnp.max(scores, axis=-1), score_new)
    weights = jnp.exp(scores - top_score[..., None])
    weight_new = jnp.exp(score_new - top_score)
    total = jnp.sum(weights, axis=-1) + weight_new
    summed = jnp.einsum(
        "rkgp,rpkd->rkgd",
        weights.astype(jnp.bfloat16),
        value_heads,
        preferred_element_type=jnp.float32,
    )
    new_low = weight_new.astype(jnp.bfloat16).astype(jnp.float32)
    summed = summed + new_low[..., None] * new_value.astype(jnp.float32).reshape(
        row_count, KVH, 1, HD
    )
    return (summed / total[..., None]).astype(jnp.bfloat16).reshape(row_count, HQ * HD)


def places():
    table = np.zeros((256, 29), np.int32)
    for device in range(256):
        x, l, y, z, core = device >> 6, (device >> 5) & 1, (device >> 3) & 3, (device >> 1) & 3, device & 1
        owners = [(z + t) % 4 for t in range(4)]
        table[device, :8] = [((x + t) % 4) * 2 + (l ^ b) for t in range(4) for b in range(2)]
        table[device, 8:12] = [(y + t) % 4 for t in range(4)]
        table[device, 12] = core
        table[device, 13:17] = [(y + t - z) % 4 for t in range(4)]
        table[device, 17:25] = [(2 * (owner % 2) + source - y) % 4 for owner in owners for source in range(2)]
        table[device, 25:29] = [owner // 2 for owner in owners]
    return table


def swap(block, axis):
    return lax.ppermute(block, axis, [(0, 1), (1, 0)])


def ring_from(block, axis, shift):
    return lax.ppermute(block, axis, [((i + shift) % 4, i) for i in range(4)])


def ring_to(block, axis, shift):
    return lax.ppermute(block, axis, [(i, (i + shift) % 4) for i in range(4)])


def params(mebibytes, flops, nbytes):
    return dict(
        compiler_params=pltpu.CompilerParams(vmem_limit_bytes=mebibytes << 20),
        cost_estimate=pl.CostEstimate(flops=flops, bytes_accessed=nbytes, transcendentals=0),
    )


def steps(width):
    return [(n, min(STEP, width - n)) for n in range(0, width, STEP)]


def start_all(copies):
    for copy in copies:
        copy.start()
    return copies


def wait_all(copies):
    for copy in copies:
        copy.wait()


def activate_kernel(*refs):
    parts, out_ref, held, hidden_ref, sems = refs[:2], refs[2], refs[3:5], refs[5], refs[6]
    copies = start_all([pltpu.make_async_copy(parts[i], held[i], sems.at[i]) for i in range(2)])
    width = hidden_ref.shape[1] // 2
    start = 0
    for i in range(2):
        copies[i].wait()
        groups, rows = held[i].shape[:2]

        def summed(first, size):
            return add_up([held[i][g, :, first : first + size] for g in range(groups)])

        square_sum = jnp.sum(summed(4 * width, 128), axis=1, keepdims=True)
        inv_rms = lax.rsqrt(square_sum / D + 1e-05)
        for j in range(2):
            for n, size in steps(width):
                gate = summed(2 * j * width + n, size) * inv_rms
                up_proj = summed((2 * j + 1) * width + n, size) * inv_rms
                hidden = gate / (1.0 + jnp.exp(-gate)) * up_proj
                hidden_ref[start : start + rows, j * width + n : j * width + n + size] = hidden.astype(jnp.bfloat16)
        start += rows
    wait_all(
        start_all(
            [pltpu.make_async_copy(hidden_ref, out_ref.at[g], sems.at[2 + g]) for g in range(out_ref.shape[0])]
        )
    )


def activate(parts):
    groups, _, width = parts[0].shape
    width = (width - 128) // 2
    rows = parts[0].shape[1] + parts[1].shape[1]
    return pl.pallas_call(
        activate_kernel,
        in_specs=[ANY] * 2,
        out_specs=ANY,
        out_shape=jax.ShapeDtypeStruct((groups, rows, width), jnp.bfloat16),
        scratch_shapes=[pltpu.VMEM(part.shape, jnp.bfloat16) for part in parts]
        + [pltpu.VMEM((rows, width), jnp.bfloat16), pltpu.SemaphoreType.DMA((2 + groups,))],
        name="activate",
        **params(12, 0, 6 * groups * rows * width),
    )(*parts)


def project_kernel(place_ref, *refs):
    pieces, own, other = refs[:4], refs[4:8], refs[8:12]
    out_ref, rows_ref, held_ref, row_sems, held_sems = refs[12:]
    step = pieces[0].shape[0] // 2
    row_copies = start_all(
        [
            pltpu.make_async_copy(
                pieces[j].at[pl.ds(b * step, step), :],
                rows_ref.at[pl.ds(pl.multiple_of(place_ref[2 * j + b] * step, step), step), :],
                row_sems.at[2 * j + b],
            )
            for j in range(4)
            for b in range(2)
        ]
    )
    depth, width = own[0].shape
    held_copies = []
    for t in range(4):
        for b in range(2):
            source = own[t] if b == 0 else other[t]
            start = (2 * place_ref[8 + t] + (place_ref[12] if b == 0 else 1 - place_ref[12])) * depth
            held = held_ref.at[pl.ds(pl.multiple_of(start, depth), depth), :]
            held_copies.append(pltpu.make_async_copy(source, held, held_sems.at[2 * t + b]))
    start_all(held_copies)
    wait_all(row_copies)
    wait_all(held_copies)
    for n, size in steps(width):
        out_ref[:, n : n + size] = jnp.dot(
            rows_ref[...], held_ref[:, n : n + size], preferred_element_type=jnp.float32
        ).astype(out_ref.dtype)


def project(place, pieces, own, other):
    count, depth = 4 * pieces[0].shape[0], pieces[0].shape[1]
    width = own[0].shape[1]
    return pl.pallas_call(
        project_kernel,
        in_specs=[SMEM] + [ANY] * 12,
        out_specs=VMEM,
        out_shape=jax.ShapeDtypeStruct((count, width), jnp.bfloat16),
        scratch_shapes=[
            pltpu.VMEM((count, depth), jnp.bfloat16),
            pltpu.VMEM((depth, width), jnp.bfloat16),
            pltpu.SemaphoreType.DMA((8,)),
            pltpu.SemaphoreType.DMA((8,)),
        ],
        name="project",
        **params(12, 2 * count * depth * width, 2 * (depth * width + count * (depth + width))),
    )(place, *pieces, *own, *other)


def gate_up_kernel(gain_ref, *refs):
    pieces, weights = refs[:-9], refs[-9:-5]
    out_ref, rows_ref, held_ref, row_sems, held_sems = refs[-5:]
    step = pieces[0].shape[0]
    width = weights[0].shape[1]
    row_copies = start_all(
        [
            pltpu.make_async_copy(piece, rows_ref.at[pl.ds(t * step, step), :], row_sems.at[t])
            for t, piece in enumerate(pieces)
        ]
    )
    held_copies = start_all(
        [pltpu.make_async_copy(weights[j], held_ref.at[j], held_sems.at[j]) for j in range(4)]
    )
    inverse = 1.0 / gain_ref[...]
    part = 64
    lane = lax.broadcasted_iota(jnp.int32, (part, 128), 1)
    wait_all(row_copies)
    for t in range(0, rows_ref.shape[0], part):
        mixed = rows_ref[t : t + part, :].astype(jnp.float32) * inverse
        squares = jnp.sum(mixed * mixed, axis=1, keepdims=True)
        high = squares.astype(jnp.bfloat16).astype(jnp.float32)
        columns = jnp.where(lane == 0, high, jnp.where(lane == 1, squares - high, 0.0))
        out_ref[t : t + part, 4 * width :] = columns.astype(out_ref.dtype)
    for j in range(4):
        held_copies[j].wait()
        for n, size in steps(width):
            product = jnp.dot(rows_ref[...], held_ref[j, :, n : n + size], preferred_element_type=jnp.float32)
            out_ref[:, j * width + n : j * width + n + size] = product.astype(out_ref.dtype)


def gate_up(gain, pieces, weights, hidden_us):
    count, depth = len(pieces) * pieces[0].shape[0], pieces[0].shape[1]
    width = weights[0].shape[1]
    return pl.pallas_call(
        gate_up_kernel,
        in_specs=[VMEM] + [ANY] * (len(pieces) + 4),
        out_specs=VMEM,
        out_shape=jax.ShapeDtypeStruct((count, 4 * width + 128), jnp.bfloat16),
        scratch_shapes=[
            pltpu.VMEM((count, depth), jnp.bfloat16),
            pltpu.VMEM((4, depth, width), jnp.bfloat16),
            pltpu.SemaphoreType.DMA((len(pieces),)),
            pltpu.SemaphoreType.DMA((4,)),
        ],
        name="gate_up",
        **params(20, hidden_us * 1153500000, 2 * (count * depth + 4 * depth * width + 4 * count * width)),
    )(gain, *pieces, *weights)


def down_kernel(place_ref, hidden_ref, own, other, mixed_ref, *refs):
    outs, rows_ref, held_ref, total_ref, row_sem, held_sems = refs[:4], *refs[4:]
    depth, width = own.shape
    row_copy = pltpu.make_async_copy(hidden_ref, rows_ref, row_sem.at[0])
    row_copy.start()
    held_copies = start_all(
        [
            pltpu.make_async_copy(weight, held_ref.at[pl.ds(i * depth, depth), :], held_sems.at[i])
            for i, weight in enumerate((own, other))
        ]
    )
    row_copy.wait()
    share = mixed_ref.shape[0]
    first = hidden_ref.shape[1] // 4
    near = rows_ref[:, :first].reshape(4 * share, 2 * depth)
    far = rows_ref[:, first:].reshape(12 * share, 2 * depth)
    wait_all(held_copies)
    for n, size in steps(width):
        columns = held_ref[:, n : n + size]
        product = jnp.dot(near, columns, preferred_element_type=jnp.float32)
        total_ref[:4, :, n : n + size] = product.reshape(4, share, size)
        product = jnp.dot(far, columns, preferred_element_type=jnp.float32)
        total_ref[4:, :, n : n + size] = product.reshape(12, share, size)
    total_ref[0] += mixed_ref[...]
    half = share // 2
    for t in range(4):
        for u in range(4):
            inner = pl.ds(pl.multiple_of(place_ref[25 + u] * half, half), half)
            for source in range(2):
                holder = place_ref[17 + 2 * u + source] * 4 + place_ref[13 + t]
                start = (2 * u + source) * half
                outs[t][start : start + half, :] = total_ref[holder, inner, :].astype(outs[t].dtype)


def down(place, hidden, weights, mixed):
    count = hidden.shape[0] * hidden.shape[1]
    depth, width = weights[0].shape
    return pl.pallas_call(
        down_kernel,
        in_specs=[SMEM] + [ANY] * 3 + [VMEM],
        out_specs=[VMEM] * 4,
        out_shape=[jax.ShapeDtypeStruct((count // 4, width), jnp.bfloat16)] * 4,
        scratch_shapes=[
            pltpu.VMEM(hidden.shape, jnp.bfloat16),
            pltpu.VMEM((2 * depth, width), jnp.bfloat16),
            pltpu.VMEM((16, count // 16, width), jnp.float32),
            pltpu.SemaphoreType.DMA((1,)),
            pltpu.SemaphoreType.DMA((2,)),
        ],
        name="down",
        **params(60, 4 * count * depth * width, 2 * (2 * count * depth + 2 * depth * width + count * width)),
    )(place, hidden, *weights, mixed)


def add_up(pieces):
    total = pieces[0].astype(jnp.float32)
    for piece in pieces[1:]:
        total = total + piece.astype(jnp.float32)
    return total


def exchange(pieces, axis):
    return lax.all_to_all(pieces, axis, split_axis=0, concat_axis=0, tiled=True)


def scatter_sum(partial, axis):
    parts = lax.axis_size(axis)
    pieces = partial.reshape(parts, partial.shape[0] // parts, partial.shape[1])
    return jnp.sum(exchange(pieces, axis).astype(jnp.float32), axis=0)


def body(
    hidden_in,
    queries,
    cache_key,
    cache_value,
    new_key,
    new_value,
    lengths,
    out_weight,
    norm_gain,
    w_gate,
    w_up,
    w_down,
):
    device = lax.axis_index(GRP + ATT)
    place = lax.dynamic_slice_in_dim(jnp.asarray(places()), device, 1, 0)[0]
    out_own = [out_weight] + [ring_from(out_weight, "y", t) for t in (1, 2, 3)]
    out_other = swap(out_weight, "core")

    attended = attend(queries, cache_key, cache_value, new_key, new_value, lengths)
    count = attended.shape[0]
    slots = attended.reshape(count, 4, 4, -1).transpose(2, 0, 1, 3).reshape(4, count, -1)
    block = exchange(slots, "z").reshape(4 * count, -1)
    block, out_own[1], out_own[3] = lax.optimization_barrier((block, out_own[1], out_own[3]))
    out_next, out_last = swap(out_own[1], "core"), swap(out_own[3], "core")
    block = jnp.concatenate([block, swap(block, "l")], axis=0)
    pieces = [block] + [ring_from(block, "x", t) for t in (1, 2, 3)]
    *pieces, out_own[2] = lax.optimization_barrier((*pieces, out_own[2]))
    partial = project(place, pieces, out_own, [out_other, out_next, swap(out_own[2], "core"), out_last])
    partial, *late = lax.optimization_barrier((partial, w_gate, w_up))
    gate_other, up_other = [swap(w, "core") for w in late]

    share = hidden_in.shape[0] // 32
    y, z, core = (device >> 3) & 3, (device >> 1) & 3, device & 1
    start = 256 * z + 32 * y
    own_in = jnp.stack([lax.dynamic_slice_in_dim(hidden_in, start + 128 * l, share, 0) for l in range(2)])
    own_in = lax.dynamic_index_in_dim(own_in.reshape(2, 4, 2, count, -1), core, 2, keepdims=False).reshape(share, -1)
    mixed = own_in.astype(jnp.float32) + scatter_sum(partial, "z")
    normed = (mixed * norm_gain).astype(jnp.bfloat16)
    normed, gate_other, up_other = lax.optimization_barrier((normed, gate_other, up_other))

    block = jnp.concatenate([normed] + [ring_from(normed, "z", t) for t in (1, 2, 3)], axis=0)
    block, late = lax.optimization_barrier((block, w_down))
    down_other = swap(late, "core")
    pieces = [ring_from(block, "y", t) for t in (1, 2, 3)]
    weights = [w_gate, w_up, gate_other, up_other]
    summed = [
        exchange(gate_up(norm_gain[None, :], part, weights, hidden_us).reshape(8, -1, 4 * w_gate.shape[1] + 128), GRP)
        for part, hidden_us in (([block], 15), (pieces, 60))
    ]
    hidden = exchange(activate(summed), GRP)
    parts = down(place, hidden, [w_down, down_other], mixed)
    total = add_up([parts[0]] + [ring_to(parts[t], "y", t) for t in (1, 2, 3)])
    parts = [total[t * share : (t + 1) * share] for t in range(4)]
    total = add_up([parts[0]] + [ring_to(parts[t].astype(jnp.bfloat16), "z", t) for t in (1, 2, 3)])
    total = total.astype(jnp.bfloat16)
    half = share // 2
    low, high = total[:half], total[half:]
    given = swap(jnp.where(core == 0, high, low), "core")
    rows = jnp.stack([jnp.where(core == 0, low, given), jnp.where(core == 0, given, high)])
    return rows.reshape(2, 4, count, -1).transpose(1, 0, 2, 3).reshape(share, -1)


def solution(mesh):
    fine = Mesh(mesh.devices.reshape(SIZES), NAMES)
    rows = P(GRP + ATT)
    in_specs = (
        P(None, GRP),
        rows,
        rows,
        rows,
        rows,
        rows,
        rows,
        P(ATT, GRP),
        P(GRP),
        P(GRP, ATT),
        P(GRP, ATT),
        P(ATT, GRP),
    )
    out_specs = P(ATT, GRP)
    return jax.shard_map(body, mesh=fine, in_specs=in_specs, out_specs=out_specs, check_vma=False)
```

```python
import jax
import jax.numpy as jnp
import numpy as np
from jax import lax
from jax.experimental import pallas as pl
from jax.experimental.pallas import tpu as pltpu
from jax.sharding import Mesh
from jax.sharding import PartitionSpec as P

NAMES = ("x", "l", "y", "z", "core")
SIZES = (4, 2, 4, 4, 2)
GRP, ATT = ("x", "l"), ("y", "z", "core")
VMEM = pl.BlockSpec(memory_space=pltpu.VMEM)
SMEM = pl.BlockSpec(memory_space=pltpu.SMEM)
ANY = pl.BlockSpec(memory_space=pl.ANY)
STEP = 256

D = 8192
HQ = 64
KVH = 8
HD = 128


def attend(queries, cache_key, cache_value, new_key, new_value, lengths):
    row_count = queries.shape[0]
    slot_count = cache_key.shape[1]
    scale_factor = 1.0 / jnp.sqrt(jnp.float32(HD))
    query_heads = queries.reshape(row_count, KVH, HQ // KVH, HD)
    key_heads = cache_key.reshape(row_count, slot_count, KVH, HD)
    value_heads = cache_value.reshape(row_count, slot_count, KVH, HD)
    scores = (
        jnp.einsum("rkgd,rpkd->rkgp", query_heads, key_heads, preferred_element_type=jnp.float32)
        * scale_factor
    )
    score_new = (
        jnp.einsum(
            "rkgd,rkd->rkg",
            query_heads,
            new_key.reshape(row_count, KVH, HD),
            preferred_element_type=jnp.float32,
        )
        * scale_factor
    )
    valid = jnp.arange(slot_count, dtype=jnp.int32)[None, :] < lengths[:, None]
    scores = jnp.where(valid[:, None, None, :], scores, -jnp.inf)
    top_score = jnp.maximum(jnp.max(scores, axis=-1), score_new)
    weights = jnp.exp(scores - top_score[..., None])
    weight_new = jnp.exp(score_new - top_score)
    total = jnp.sum(weights, axis=-1) + weight_new
    summed = jnp.einsum(
        "rkgp,rpkd->rkgd",
        weights.astype(jnp.bfloat16),
        value_heads,
        preferred_element_type=jnp.float32,
    )
    new_low = weight_new.astype(jnp.bfloat16).astype(jnp.float32)
    summed = summed + new_low[..., None] * new_value.astype(jnp.float32).reshape(
        row_count, KVH, 1, HD
    )
    return (summed / total[..., None]).astype(jnp.bfloat16).reshape(row_count, HQ * HD)


def places():
    table = np.zeros((256, 29), np.int32)
    for device in range(256):
        x, l, y, z, core = device >> 6, (device >> 5) & 1, (device >> 3) & 3, (device >> 1) & 3, device & 1
        owners = [(z + t) % 4 for t in range(4)]
        table[device, :8] = [((x + t) % 4) * 2 + (l ^ b) for t in range(4) for b in range(2)]
        table[device, 8:12] = [(y + t) % 4 for t in range(4)]
        table[device, 12] = core
        table[device, 13:17] = [(y + t - z) % 4 for t in range(4)]
        table[device, 17:25] = [(2 * (owner % 2) + source - y) % 4 for owner in owners for source in range(2)]
        table[device, 25:29] = [owner // 2 for owner in owners]
    return table


def swap(block, axis):
    return lax.ppermute(block, axis, [(0, 1), (1, 0)])


def ring_from(block, axis, shift):
    return lax.ppermute(block, axis, [((i + shift) % 4, i) for i in range(4)])


def ring_to(block, axis, shift):
    return lax.ppermute(block, axis, [(i, (i + shift) % 4) for i in range(4)])


def params(mebibytes, flops, nbytes):
    return dict(
        compiler_params=pltpu.CompilerParams(vmem_limit_bytes=mebibytes << 20),
        cost_estimate=pl.CostEstimate(flops=flops, bytes_accessed=nbytes, transcendentals=0),
    )


def steps(width):
    return [(n, min(STEP, width - n)) for n in range(0, width, STEP)]


def start_all(copies):
    for copy in copies:
        copy.start()
    return copies


def wait_all(copies):
    for copy in copies:
        copy.wait()


def activate_kernel(*refs):
    parts, out_ref, held, hidden_ref, sems = refs[:2], refs[2], refs[3:5], refs[5], refs[6]
    copies = start_all([pltpu.make_async_copy(parts[i], held[i], sems.at[i]) for i in range(2)])
    width = hidden_ref.shape[1] // 2
    start = 0
    for i in range(2):
        copies[i].wait()
        groups, rows = held[i].shape[:2]

        def summed(first, size):
            return add_up([held[i][g, :, first : first + size] for g in range(groups)])

        square_sum = jnp.sum(summed(4 * width, 128), axis=1, keepdims=True)
        inv_rms = lax.rsqrt(square_sum / D + 1e-05)
        for j in range(2):
            for n, size in steps(width):
                gate = summed(2 * j * width + n, size) * inv_rms
                up_proj = summed((2 * j + 1) * width + n, size) * inv_rms
                hidden = gate / (1.0 + jnp.exp(-gate)) * up_proj
                hidden_ref[start : start + rows, j * width + n : j * width + n + size] = hidden.astype(jnp.bfloat16)
        start += rows
    wait_all(
        start_all(
            [pltpu.make_async_copy(hidden_ref, out_ref.at[g], sems.at[2 + g]) for g in range(out_ref.shape[0])]
        )
    )


def activate(parts):
    groups, _, width = parts[0].shape
    width = (width - 128) // 2
    rows = parts[0].shape[1] + parts[1].shape[1]
    return pl.pallas_call(
        activate_kernel,
        in_specs=[ANY] * 2,
        out_specs=ANY,
        out_shape=jax.ShapeDtypeStruct((groups, rows, width), jnp.bfloat16),
        scratch_shapes=[pltpu.VMEM(part.shape, jnp.bfloat16) for part in parts]
        + [pltpu.VMEM((rows, width), jnp.bfloat16), pltpu.SemaphoreType.DMA((2 + groups,))],
        name="activate",
        **params(60, 0, 6 * groups * rows * width),
    )(*parts)


def project_kernel(place_ref, *refs):
    pieces, own, other = refs[:4], refs[4:8], refs[8:12]
    out_ref, rows_ref, held_ref, row_sems, held_sems = refs[12:]
    step = pieces[0].shape[0] // 2
    row_copies = start_all(
        [
            pltpu.make_async_copy(
                pieces[j].at[pl.ds(b * step, step), :],
                rows_ref.at[pl.ds(pl.multiple_of(place_ref[2 * j + b] * step, step), step), :],
                row_sems.at[2 * j + b],
            )
            for j in range(4)
            for b in range(2)
        ]
    )
    depth, width = own[0].shape
    held_copies = []
    for t in range(4):
        for b in range(2):
            source = own[t] if b == 0 else other[t]
            start = (2 * place_ref[8 + t] + (place_ref[12] if b == 0 else 1 - place_ref[12])) * depth
            held = held_ref.at[pl.ds(pl.multiple_of(start, depth), depth), :]
            held_copies.append(pltpu.make_async_copy(source, held, held_sems.at[2 * t + b]))
    start_all(held_copies)
    wait_all(row_copies)
    wait_all(held_copies)
    for n, size in steps(width):
        out_ref[:, n : n + size] = jnp.dot(
            rows_ref[...], held_ref[:, n : n + size], preferred_element_type=jnp.float32
        ).astype(out_ref.dtype)


def project(place, pieces, own, other):
    count, depth = 4 * pieces[0].shape[0], pieces[0].shape[1]
    width = own[0].shape[1]
    return pl.pallas_call(
        project_kernel,
        in_specs=[SMEM] + [ANY] * 12,
        out_specs=VMEM,
        out_shape=jax.ShapeDtypeStruct((count, width), jnp.bfloat16),
        scratch_shapes=[
            pltpu.VMEM((count, depth), jnp.bfloat16),
            pltpu.VMEM((depth, width), jnp.bfloat16),
            pltpu.SemaphoreType.DMA((8,)),
            pltpu.SemaphoreType.DMA((8,)),
        ],
        name="project",
        **params(12, 2 * count * depth * width, 2 * (depth * width + count * (depth + width))),
    )(place, *pieces, *own, *other)


def gate_up_kernel(gain_ref, *refs):
    pieces, weights = refs[:-9], refs[-9:-5]
    out_ref, rows_ref, held_ref, row_sems, held_sems = refs[-5:]
    step = pieces[0].shape[0]
    width = weights[0].shape[1]
    row_copies = start_all(
        [
            pltpu.make_async_copy(piece, rows_ref.at[pl.ds(t * step, step), :], row_sems.at[t])
            for t, piece in enumerate(pieces)
        ]
    )
    held_copies = start_all(
        [pltpu.make_async_copy(weights[j], held_ref.at[j], held_sems.at[j]) for j in range(4)]
    )
    inverse = 1.0 / gain_ref[...]
    part = 64
    lane = lax.broadcasted_iota(jnp.int32, (part, 128), 1)
    wait_all(row_copies)
    for t in range(0, rows_ref.shape[0], part):
        mixed = rows_ref[t : t + part, :].astype(jnp.float32) * inverse
        squares = jnp.sum(mixed * mixed, axis=1, keepdims=True)
        high = squares.astype(jnp.bfloat16).astype(jnp.float32)
        columns = jnp.where(lane == 0, high, jnp.where(lane == 1, squares - high, 0.0))
        out_ref[t : t + part, 4 * width :] = columns.astype(out_ref.dtype)
    for j in range(4):
        held_copies[j].wait()
        for n, size in steps(width):
            product = jnp.dot(rows_ref[...], held_ref[j, :, n : n + size], preferred_element_type=jnp.float32)
            out_ref[:, j * width + n : j * width + n + size] = product.astype(out_ref.dtype)


def gate_up(gain, pieces, weights, hidden_us):
    count, depth = len(pieces) * pieces[0].shape[0], pieces[0].shape[1]
    width = weights[0].shape[1]
    return pl.pallas_call(
        gate_up_kernel,
        in_specs=[VMEM] + [ANY] * (len(pieces) + 4),
        out_specs=VMEM,
        out_shape=jax.ShapeDtypeStruct((count, 4 * width + 128), jnp.bfloat16),
        scratch_shapes=[
            pltpu.VMEM((count, depth), jnp.bfloat16),
            pltpu.VMEM((4, depth, width), jnp.bfloat16),
            pltpu.SemaphoreType.DMA((len(pieces),)),
            pltpu.SemaphoreType.DMA((4,)),
        ],
        name="gate_up",
        **params(20, hidden_us * 1153500000, 2 * (count * depth + 4 * depth * width + 4 * count * width)),
    )(gain, *pieces, *weights)


def down_kernel(place_ref, hidden_ref, own, other, mixed_ref, *refs):
    outs, rows_ref, held_ref, total_ref, row_sem, held_sems = refs[:4], *refs[4:]
    depth, width = own.shape
    row_copy = pltpu.make_async_copy(hidden_ref, rows_ref, row_sem.at[0])
    row_copy.start()
    held_copies = start_all(
        [
            pltpu.make_async_copy(weight, held_ref.at[pl.ds(i * depth, depth), :], held_sems.at[i])
            for i, weight in enumerate((own, other))
        ]
    )
    row_copy.wait()
    share = mixed_ref.shape[0]
    first = hidden_ref.shape[1] // 4
    near = rows_ref[:, :first].reshape(4 * share, 2 * depth)
    far = rows_ref[:, first:].reshape(12 * share, 2 * depth)
    wait_all(held_copies)
    for n, size in steps(width):
        columns = held_ref[:, n : n + size]
        product = jnp.dot(near, columns, preferred_element_type=jnp.float32)
        total_ref[:4, :, n : n + size] = product.reshape(4, share, size)
        product = jnp.dot(far, columns, preferred_element_type=jnp.float32)
        total_ref[4:, :, n : n + size] = product.reshape(12, share, size)
    total_ref[0] += mixed_ref[...]
    half = share // 2
    for t in range(4):
        for u in range(4):
            inner = pl.ds(pl.multiple_of(place_ref[25 + u] * half, half), half)
            for source in range(2):
                holder = place_ref[17 + 2 * u + source] * 4 + place_ref[13 + t]
                start = (2 * u + source) * half
                outs[t][start : start + half, :] = total_ref[holder, inner, :].astype(outs[t].dtype)


def down(place, hidden, weights, mixed):
    count = hidden.shape[0] * hidden.shape[1]
    depth, width = weights[0].shape
    return pl.pallas_call(
        down_kernel,
        in_specs=[SMEM] + [ANY] * 3 + [VMEM],
        out_specs=[VMEM] * 4,
        out_shape=[jax.ShapeDtypeStruct((count // 4, width), jnp.bfloat16)] * 4,
        scratch_shapes=[
            pltpu.VMEM(hidden.shape, jnp.bfloat16),
            pltpu.VMEM((2 * depth, width), jnp.bfloat16),
            pltpu.VMEM((16, count // 16, width), jnp.float32),
            pltpu.SemaphoreType.DMA((1,)),
            pltpu.SemaphoreType.DMA((2,)),
        ],
        name="down",
        **params(60, 4 * count * depth * width, 2 * (2 * count * depth + 2 * depth * width + count * width)),
    )(place, hidden, *weights, mixed)


def add_up(pieces):
    total = pieces[0].astype(jnp.float32)
    for piece in pieces[1:]:
        total = total + piece.astype(jnp.float32)
    return total


def exchange(pieces, axis):
    return lax.all_to_all(pieces, axis, split_axis=0, concat_axis=0, tiled=True)


def scatter_sum(partial, axis):
    parts = lax.axis_size(axis)
    pieces = partial.reshape(parts, partial.shape[0] // parts, partial.shape[1])
    return jnp.sum(exchange(pieces, axis).astype(jnp.float32), axis=0)


def body(
    hidden_in,
    queries,
    cache_key,
    cache_value,
    new_key,
    new_value,
    lengths,
    out_weight,
    norm_gain,
    w_gate,
    w_up,
    w_down,
):
    device = lax.axis_index(GRP + ATT)
    place = lax.dynamic_slice_in_dim(jnp.asarray(places()), device, 1, 0)[0]
    out_own = [out_weight] + [ring_from(out_weight, "y", t) for t in (1, 2, 3)]
    out_other = swap(out_weight, "core")

    attended = attend(queries, cache_key, cache_value, new_key, new_value, lengths)
    count = attended.shape[0]
    slots = attended.reshape(count, 4, 4, -1).transpose(2, 0, 1, 3).reshape(4, count, -1)
    block = exchange(slots, "z").reshape(4 * count, -1)
    block, out_own[1], out_own[3] = lax.optimization_barrier((block, out_own[1], out_own[3]))
    out_next, out_last = swap(out_own[1], "core"), swap(out_own[3], "core")
    block = jnp.concatenate([block, swap(block, "l")], axis=0)
    pieces = [block] + [ring_from(block, "x", t) for t in (1, 2, 3)]
    *pieces, out_own[2] = lax.optimization_barrier((*pieces, out_own[2]))
    partial = project(place, pieces, out_own, [out_other, out_next, swap(out_own[2], "core"), out_last])
    partial, *late = lax.optimization_barrier((partial, w_gate, w_up))
    gate_other, up_other = [swap(w, "core") for w in late]

    share = hidden_in.shape[0] // 32
    y, z, core = (device >> 3) & 3, (device >> 1) & 3, device & 1
    start = 256 * z + 32 * y
    own_in = jnp.stack([lax.dynamic_slice_in_dim(hidden_in, start + 128 * l, share, 0) for l in range(2)])
    own_in = lax.dynamic_index_in_dim(own_in.reshape(2, 4, 2, count, -1), core, 2, keepdims=False).reshape(share, -1)
    mixed = own_in.astype(jnp.float32) + scatter_sum(partial, "z")
    normed = (mixed * norm_gain).astype(jnp.bfloat16)
    normed, gate_other, up_other = lax.optimization_barrier((normed, gate_other, up_other))

    block = jnp.concatenate([normed] + [ring_from(normed, "z", t) for t in (1, 2, 3)], axis=0)
    block, late = lax.optimization_barrier((block, w_down))
    down_other = swap(late, "core")
    pieces = [ring_from(block, "y", t) for t in (1, 2, 3)]
    weights = [w_gate, w_up, gate_other, up_other]
    summed = [
        exchange(gate_up(norm_gain[None, :], part, weights, hidden_us).reshape(8, -1, 4 * w_gate.shape[1] + 128), GRP)
        for part, hidden_us in (([block], 15), (pieces, 60))
    ]
    hidden = exchange(activate(summed), GRP)
    parts = down(place, hidden, [w_down, down_other], mixed)
    total = add_up([parts[0]] + [ring_to(parts[t], "y", t) for t in (1, 2, 3)])
    parts = [total[t * share : (t + 1) * share] for t in range(4)]
    total = add_up([parts[0]] + [ring_to(parts[t].astype(jnp.bfloat16), "z", t) for t in (1, 2, 3)])
    total = total.astype(jnp.bfloat16)
    half = share // 2
    low, high = total[:half], total[half:]
    given = swap(jnp.where(core == 0, high, low), "core")
    rows = jnp.stack([jnp.where(core == 0, low, given), jnp.where(core == 0, given, high)])
    return rows.reshape(2, 4, count, -1).transpose(1, 0, 2, 3).reshape(share, -1)


def solution(mesh):
    fine = Mesh(mesh.devices.reshape(SIZES), NAMES)
    rows = P(GRP + ATT)
    in_specs = (
        P(None, GRP),
        rows,
        rows,
        rows,
        rows,
        rows,
        rows,
        P(ATT, GRP),
        P(GRP),
        P(GRP, ATT),
        P(GRP, ATT),
        P(ATT, GRP),
    )
    out_specs = P(ATT, GRP)
    return jax.shard_map(body, mesh=fine, in_specs=in_specs, out_specs=out_specs, check_vma=False)
```
